256 devices in a mesh: dp: 8 (over y, core), proto: 32 (over z, x).
Axes of the slice: x: 4, y: 4, z: 8, core: 2. Of those that a mesh axis runs over, the one named last changes fastest.
Arguments:
- student_rows: bfloat16 [128, 256, 256], P('dp'), may hold values from -0.375 to 0.375
- teacher_rows: bfloat16 [128, 256, 256], P('dp'), may hold values from -0.375 to 0.375
- student_proto: bfloat16 [256, 131072], P(None, 'proto'), may hold values from -0.375 to 0.375
- teacher_proto: bfloat16 [256, 131072], P(None, 'proto'), may hold values from -0.375 to 0.375
- center: float32 [131072], P('proto'), may hold values from -0.05 to 0.05
- counts: int32 [128], replicated, may hold values from 1 to 128, 12288 in all
- mask_order: int32 [128, 256], P('dp'), may hold values from 0 to 255, each once within a row
Outputs:
- row_loss: float32 [8, 1536], P('dp')
- student_grad: bfloat16 [8, 1536, 256], P('dp')
The draws below stay inside these ranges and needn't reach their ends.
Inputs may be any that keep to these rules, and one draw needn't show every extreme that they name: counts sum to 12288, and some image has exactly 128. `mask_order`: each row is a permutation of the patch positions; image i's masked patches are its first counts[i] entries.
All inputs are finite; a program needn't handle non-finite values.
Results may differ from the reference program's by a relative error of at most 0.002.
The reference program's roundings to bfloat16 on the way count: a program that leaves them out, or rounds other values in their place, can miss the bound.
Values may be sent and summed in bfloat16 or wider, within the bound.
A program may use at most 192 MiB of HBM per device.

```python
import math
import jax
import jax.numpy as jnp
import numpy as np
from jax import lax

E = 256
PROTOS = 131072
PATCHES = 256
MASK_IMG = 96
MAXM = 128
IMAGES = 128
MASK_DEV = 1536
N_DP = 8
N_PROTO = 32


def shard_levels(stream_key, shape, split, low, high):
    gain = 1.0
    for axis_at, blocks in split:
        steps = jax.random.uniform(jax.random.fold_in(jax.random.fold_in(stream_key, 6), axis_at), (blocks,), jnp.float32, low / len(split), high / len(split))
        gain = gain * jnp.repeat(jnp.exp(steps), shape[axis_at] // blocks).reshape((-1,) + (1,) * (len(shape) - 1 - axis_at))
    return gain


def profile(count, total, limit, skew):
    loads = [(1 << 20) // math.isqrt(standing ** skew) + 1 for standing in range(2, count + 1)]
    surplus, holding = total - limit - (count - 1), [1] * (count - 1)
    while surplus > 0:
        free = [i for i in range(count - 1) if holding[i] < limit]
        whole, remaining = sum([loads[i] for i in free]), surplus
        for i in free:
            extra = min(limit - holding[i], max(1, remaining * loads[i] // whole), surplus)
            holding[i] = holding[i] + extra
            surplus = surplus - extra
    return np.array([limit] + holding)


def ragged_sizes(own_key, count, total, most, slope):
    if count == 2:
        one = jax.random.randint(own_key, (), max(1, total - most), min(most, total - 1) + 1)
        return jnp.stack([one, total - one])
    tallies = jnp.asarray(profile(count, total, most, slope), jnp.int32)
    twos = (count - 1) // 2
    donor, receiver = tallies[1:1 + 2 * twos:2], tallies[2:2 + 2 * twos:2]
    margin = jnp.minimum(donor - 1, most - receiver)
    moved = jax.random.randint(jax.random.fold_in(own_key, 1), (twos,), 0, 1 << 20) % (margin + 1)
    tallies = tallies.at[1:1 + 2 * twos:2].set(donor - moved).at[2:2 + 2 * twos:2].set(receiver + moved)
    return tallies[jax.random.permutation(jax.random.fold_in(own_key, 2), count)]


def scatter_about(key, shape, scale, most, shards=(), kind=jnp.bfloat16):
    entries = scale * jax.random.normal(key, shape, jnp.float32)
    if shards:
        entries = entries * shard_levels(key, shape, shards, -0.22, 0.18)
    return jnp.clip(entries, -most, most).astype(kind)


def setup_inputs(seed: int = 0) -> dict:
    key_list = jax.random.split(jax.random.key(seed), 8)
    student_rows = scatter_about(key_list[0], (IMAGES, PATCHES, E), 0.0625, 0.375, ((0, 8),))
    teacher_rows = scatter_about(key_list[1], (IMAGES, PATCHES, E), 0.0625, 0.375, ((0, 8),))
    student_proto = scatter_about(key_list[2], (E, PROTOS), E ** -0.5, 0.375, ((1, 32),))
    teacher_proto = scatter_about(key_list[3], (E, PROTOS), E ** -0.5, 0.375, ((1, 32),))
    center = jnp.clip(jax.random.uniform(key_list[4], (PROTOS,), jnp.float32, -0.05, 0.05) * shard_levels(key_list[4], (PROTOS,), ((0, 32),), -0.4, 0.0), -0.05, 0.05)
    counts = ragged_sizes(key_list[5], IMAGES, MASK_IMG * IMAGES, MAXM, 2).astype(jnp.int32)
    mask_order = jax.vmap(lambda own: jax.random.permutation(own, PATCHES))(jax.random.split(key_list[6], IMAGES)).reshape((IMAGES, PATCHES)).astype(jnp.int32)
    return dict(student_rows=student_rows, teacher_rows=teacher_rows, student_proto=student_proto, teacher_proto=teacher_proto, center=center, counts=counts, mask_order=mask_order)


STUDENT_TEMP = 0.1
TEACHER_TEMP = 0.07
EPSILON = 1e-06

def reference(student_rows, teacher_rows, student_proto, teacher_proto, center, counts, mask_order):
    total_rows = MASK_IMG * IMAGES
    image_ends = jnp.cumsum(counts).astype(jnp.int32)
    image_starts = (image_ends - counts).astype(jnp.int32)
    global_pos = jnp.arange(total_rows, dtype=jnp.int32)
    image_ids = lax.optimization_barrier(jnp.sum((global_pos[:, None] >= image_ends[None, :]).astype(jnp.int32), axis=1)).astype(jnp.int32)
    within = (global_pos - image_starts[image_ids]).astype(jnp.int32)
    patch_ids = mask_order[image_ids, within]
    student_in = student_rows[image_ids, patch_ids].astype(jnp.float32)
    teacher_in = teacher_rows[image_ids, patch_ids].astype(jnp.float32)
    student_norm = jnp.sqrt(lax.optimization_barrier(jnp.sum(student_in * student_in, axis=-1, keepdims=True)) + EPSILON)
    teacher_norm = jnp.sqrt(lax.optimization_barrier(jnp.sum(teacher_in * teacher_in, axis=-1, keepdims=True)) + EPSILON)
    student_unit = (student_in / student_norm).astype(jnp.bfloat16)
    teacher_unit = (teacher_in / teacher_norm).astype(jnp.bfloat16)

    def norm_columns(weights):
        wide = weights.astype(jnp.float32)
        return (wide / jnp.sqrt(lax.optimization_barrier(jnp.sum(wide * wide, axis=0, keepdims=True)) + EPSILON)).astype(jnp.bfloat16)
    block_cols = PROTOS // N_PROTO
    student_blocks = norm_columns(student_proto).reshape(E, N_PROTO, block_cols).transpose(1, 0, 2)
    teacher_blocks = norm_columns(teacher_proto).reshape(E, N_PROTO, block_cols).transpose(1, 0, 2)
    center_blocks = center.reshape(N_PROTO, block_cols)

    def exponentials(student_block, teacher_block, center_block):
        student_logit = jnp.dot(student_unit, student_block, preferred_element_type=jnp.float32)
        teacher_logit = jnp.dot(teacher_unit, teacher_block, preferred_element_type=jnp.float32)
        student_exp = jnp.exp(student_logit / STUDENT_TEMP)
        teacher_exp = jnp.exp((teacher_logit - center_block[None, :]) / TEACHER_TEMP)
        return (student_logit, student_exp, teacher_exp)

    def statistic_pass(running, block_in):
        student_logit, student_exp, teacher_exp = exponentials(*block_in)
        return ((running[0] + lax.optimization_barrier(jnp.sum(student_exp, axis=1)), running[1] + lax.optimization_barrier(jnp.sum(teacher_exp, axis=1)), running[2] + lax.optimization_barrier(jnp.sum(teacher_exp * (student_logit / STUDENT_TEMP), axis=1))), None)
    zero_rows = jnp.zeros((total_rows,), jnp.float32)
    sums, unused = lax.scan(statistic_pass, (zero_rows, zero_rows, zero_rows), (student_blocks, teacher_blocks, center_blocks))
    student_sum, teacher_sum, cross_sum = sums
    row_losses = jnp.log(student_sum) - cross_sum / teacher_sum

    def gradient_pass(running, block_in):
        student_logit, student_exp, teacher_exp = exponentials(*block_in)
        logit_grad = ((student_exp / student_sum[:, None] - teacher_exp / teacher_sum[:, None]) / STUDENT_TEMP).astype(jnp.bfloat16)
        term = lax.dot_general(logit_grad, block_in[0], (((1,), (1,)), ((), ())), preferred_element_type=jnp.float32)
        return (running + term, None)
    feature_grad, unused = lax.scan(gradient_pass, jnp.zeros((total_rows, E), jnp.float32), (student_blocks, teacher_blocks, center_blocks))
    inner = lax.optimization_barrier(jnp.sum(student_in * feature_grad, axis=-1, keepdims=True))
    input_grad = feature_grad / student_norm - student_in * inner / (student_norm * student_norm * student_norm)
    row_loss = row_losses.reshape(MASK_DEV, N_DP).T
    student_grad = input_grad.astype(jnp.bfloat16).reshape(MASK_DEV, N_DP, E).transpose(1, 0, 2)
    return (row_loss, student_grad)
```

```python
import functools
import math

import jax
import jax.numpy as jnp
from jax import lax
from jax.experimental import pallas as pl
from jax.experimental.pallas import tpu as pltpu
from jax.sharding import PartitionSpec as P

STUDENT_TEMP = 0.1
TEACHER_TEMP = 0.07
EPSILON = 1e-06
LOG2E = math.log2(math.e)
X_SIZE = 4
F32 = jnp.float32
BF16 = jnp.bfloat16
MESH = pl.DeviceIdType.MESH
NT = (((1,), (1,)), ((), ()))
TN = (((0,), (0,)), ((), ()))


def iota(shape, dim):
    return lax.broadcasted_iota(jnp.int32, shape, dim)


def head_kernel(dims, *refs):
    ndp, nz, nx, images, slots, block = dims
    (student_hbm, teacher_hbm, sproto_hbm, tproto_hbm, center_ref, counts_ref, order_ref,
     gathered, losses,
     scols, scols_t, tcols_t, center_b, s_in, s_unit, t_unit, stat_x, stat_z, grad_x, got_x, grad_z, got_z, own_dp, got_dp,
     load_sem, sx_send, sx_recv, sz_send, sz_recv, gx_send, gx_recv, gz_send, gz_recv,
     dp_send, dp_recv, az_send, az_recv, ax_send, ax_recv, lo_send, lo_recv) = refs
    chunks = images // nx
    rows = nx * slots
    piece = slots // nz
    per_res = piece // ndp
    slot_rows = own_dp.shape[2]
    protos = scols.shape[1]
    width = scols.shape[0]
    patches = order_ref.shape[1]
    me = lax.axis_index("dp")
    q = lax.axis_index("proto")
    z = q // nx
    x = q % nx

    def along_x(d):
        return (me, z * nx + lax.rem(x + d, nx))

    def along_z(d):
        return (me, lax.rem(z + d, nz) * nx + x)

    def along_dp(d):
        return (lax.rem(me + d, ndp), q)

    barrier = pltpu.get_barrier_semaphore()
    partners = (
        [along_x(d) for d in range(1, nx)]
        + [along_z(d) for d in range(1, nz)]
        + [along_dp(d) for d in range(1, ndp)]
    )
    for partner in partners:
        pl.semaphore_signal(barrier, inc=1, device_id=partner, device_id_type=MESH)

    def prologue(srows, trows, tcols):
        loads = [
            pltpu.make_async_copy(src, dst, load_sem.at[i])
            for i, (src, dst) in enumerate(
                ((student_hbm, srows), (teacher_hbm, trows), (sproto_hbm, scols), (tproto_hbm, tcols))
            )
        ]
        for load in loads:
            load.start()

        def spread_center(n, carry):
            at = pl.ds(pl.multiple_of(n * 128, 128), 128)
            row = center_ref[:, at] * (LOG2E / TEACHER_TEMP)
            center_b[at, :] = jnp.transpose(jnp.broadcast_to(row, (128, 128)))
            return carry

        lax.fori_loop(0, protos // 128, spread_center, 0)
        loads[0].wait()
        loads[1].wait()

        def gather_image(i, carry):
            order = order_ref[pl.ds(i, 1), :][:, :slots]
            pick = (iota((patches, slots), 0) == order).astype(F32).astype(BF16)
            student = lax.dot_general(pick, srows[i], TN, preferred_element_type=F32)
            teacher = lax.dot_general(pick, trows[i], TN, preferred_element_type=F32)
            at = pl.ds(pl.multiple_of(i * slots, slots), slots)
            s_in[i] = student.astype(BF16)
            s_norm = jnp.sqrt(jnp.sum(student * student, axis=1, keepdims=True) + EPSILON)
            t_norm = jnp.sqrt(jnp.sum(teacher * teacher, axis=1, keepdims=True) + EPSILON)
            s_unit[at, :] = (student / s_norm).astype(BF16)
            t_unit[at, :] = (teacher / t_norm).astype(BF16)
            return carry

        lax.fori_loop(0, images, gather_image, 0)
        loads[2].wait()
        loads[3].wait()

        def norm_tile(n, carry):
            at = pl.ds(pl.multiple_of(n * 256, 256), 256)
            for cols, turned in ((scols, scols_t), (tcols, tcols_t)):
                wide = cols[:, at].astype(F32)
                scale = 1.0 / jnp.sqrt(jnp.sum(wide * wide, axis=0, keepdims=True) + EPSILON)
                unit = (wide * scale).astype(BF16)
                if cols is scols:
                    cols[:, at] = unit
                turned[at, :] = jnp.transpose(unit)
            return carry

        lax.fori_loop(0, protos // 256, norm_tile, 0)

    pl.run_scoped(
        prologue,
        pltpu.VMEM((images, patches, width), BF16),
        pltpu.VMEM((images, patches, width), BF16),
        pltpu.VMEM((width, protos), BF16),
    )

    def copy(src, dst, send, recv, device):
        return pltpu.make_async_remote_copy(
            src_ref=src, dst_ref=dst, send_sem=send, recv_sem=recv, device_id=device,
            device_id_type=MESH,
        )

    def stat_x_copy(c, d):
        return copy(stat_x.at[c, 0], stat_x.at[c, d], sx_send.at[c, d], sx_recv.at[c, d], along_x(d))

    def stat_z_copy(c, d):
        return copy(stat_z.at[c, 0], stat_z.at[c, d], sz_send.at[c, d], sz_recv.at[c, d], along_z(d))

    def grad_x_copy(c, d):
        return copy(
            grad_x.at[c, lax.rem(x + d, nx)], got_x.at[c, d], gx_send.at[c, d], gx_recv.at[c, d],
            along_x(d),
        )

    def grad_z_copy(c, d):
        return copy(
            grad_z.at[c, lax.rem(z + d, nz)], got_z.at[c, d], gz_send.at[c, d], gz_recv.at[c, d],
            along_z(d),
        )

    def dp_copy(c, d):
        return copy(
            own_dp.at[c, lax.rem(me + d, ndp)], got_dp.at[c, me], dp_send.at[c, d], dp_recv.at[c, d],
            along_dp(d),
        )

    def all_z_copy(c, d):
        block_ref = gathered.at[x, c, z]
        return copy(block_ref, block_ref, az_send.at[c, d], az_recv.at[c, d], along_z(d))

    def all_x_copy(c, d):
        block_ref = gathered.at[x, c]
        return copy(block_ref, block_ref, ax_send.at[c, d], ax_recv.at[c, d], along_x(d))

    def loss_copy(d):
        return copy(losses.at[me], losses.at[me], lo_send.at[d], lo_recv.at[d], along_dp(d))

    def statistics(s_exp, t_exp, c):
        slot = lax.rem(c, 2)
        at_rows = pl.ds(pl.multiple_of(c * rows, rows), rows)
        student = s_unit[at_rows, :]
        teacher = t_unit[at_rows, :]

        sums = [jnp.zeros((8, rows), F32)] * 3
        for n in range(0, protos, block):
            at = pl.ds(n, block)
            s = lax.dot_general(scols_t[at, :], student, NT, preferred_element_type=F32)
            t = lax.dot_general(tcols_t[at, :], teacher, NT, preferred_element_type=F32)
            shift = jnp.concatenate([center_b[at, :]] * (rows // 128), axis=1)
            es = jnp.exp2(s * (LOG2E / STUDENT_TEMP))
            et = jnp.exp2(t * (LOG2E / TEACHER_TEMP) - shift)
            s_exp[slot, at, :] = es
            t_exp[slot, at, :] = et
            sums = [
                total + jnp.sum(part.reshape(block // 8, 8, rows), axis=0)
                for total, part in zip(sums, (es, et, et * s))
            ]
        lines = [jnp.sum(total, axis=0, keepdims=True) for total in sums]
        stat_x[c, 0] = jnp.concatenate(lines + [jnp.zeros((1, rows), F32)], axis=0)
        for d in range(1, nx):
            stat_x_copy(c, d).start()

    def statistics_over_z(c):
        total = stat_x[c, 0]
        for d in range(1, nx):
            stat_x_copy(c, d).wait_recv()
            total = total + stat_x[c, d]
        stat_z[c, 0] = total
        for d in range(1, nz):
            stat_z_copy(c, d).start()

    def gradient(s_exp, t_exp, c):
        slot = lax.rem(c, 2)
        total = stat_z[c, 0]
        for d in range(1, nz):
            stat_z_copy(c, d).wait_recv()
            total = total + stat_z[c, d]
        s_sum, t_sum, cross = total[0:1, :], total[1:2, :], total[2:3, :]
        loss = jnp.log(s_sum) - cross * (1.0 / STUDENT_TEMP) / t_sum
        losses[me, pl.ds(c * nx, nx), :] = jnp.concatenate(
            [loss[:, i * slots : (i + 1) * slots] for i in range(nx)], axis=0
        )
        s_scale = (1.0 / STUDENT_TEMP) / s_sum
        t_scale = (1.0 / STUDENT_TEMP) / t_sum
        dz = jnp.zeros((width, rows), F32)
        for n in range(0, protos, block):
            at = pl.ds(n, block)
            dlogit = (s_exp[slot, at, :] * s_scale - t_exp[slot, at, :] * t_scale).astype(BF16)
            dz = dz + jnp.dot(scols[:, at], dlogit, preferred_element_type=F32)
        grad_x[c] = jnp.transpose(dz).reshape(nx, slots, width)
        for d in range(1, nx):
            grad_x_copy(c, d).start()

    def gradient_over_z(c):
        total = grad_x[c, x]
        for d in range(1, nx):
            grad_x_copy(c, d).wait_recv()
            total = total + got_x[c, d]
        grad_z[c] = total.reshape(nz, piece, width)
        for d in range(1, nz):
            grad_z_copy(c, d).start()

    def finish(c):
        dz = grad_z[c, z]
        for d in range(1, nz):
            grad_z_copy(c, d).wait_recv()
            dz = dz + got_z[c, d]
        image = c * nx + x
        xs = s_in[image, pl.ds(pl.multiple_of(z * piece, piece), piece), :].astype(F32)
        norm = jnp.sqrt(jnp.sum(xs * xs, axis=1, keepdims=True) + EPSILON)
        inner = jnp.sum(xs * dz, axis=1, keepdims=True)
        dx = (dz / norm - xs * inner / (norm * norm * norm)).astype(BF16)
        before = iota(counts_ref.shape, 1) < me * images + image
        start = jnp.sum(jnp.where(before, counts_ref[...].astype(F32), 0.0), axis=1, keepdims=True)
        first = jnp.broadcast_to(start.astype(jnp.int32), (ndp * slot_rows, piece))
        pos = iota((ndp * slot_rows, piece), 0)
        k = iota((ndp * slot_rows, piece), 1)
        pick = (((first + k) % ndp) == pos // slot_rows) & (k // ndp == pos % slot_rows)
        sent = jnp.dot(pick.astype(F32).astype(BF16), dx, preferred_element_type=F32)
        own_dp[c] = sent.reshape(ndp, slot_rows, width)
        for d in range(1, ndp):
            dp_copy(c, d).start()
        got_dp[c, me] = own_dp[c, me]

    def spread_z(c):
        for d in range(1, ndp):
            dp_copy(c, d).wait_recv()
        held = got_dp[c].reshape(ndp * slot_rows, width).astype(BF16)
        pos = iota((piece, ndp * slot_rows), 0)
        k = iota((piece, ndp * slot_rows), 1)
        pick = (k // slot_rows == pos // per_res) & (k % slot_rows == pos % per_res)
        gathered[x, c, z] = jnp.dot(
            pick.astype(F32).astype(BF16), held, preferred_element_type=F32
        ).astype(BF16)
        for d in range(1, nz):
            all_z_copy(c, d).start()

    def spread_x(c):
        for d in range(1, nz):
            all_z_copy(c, d).wait_recv()
        for d in range(1, nx):
            all_x_copy(c, d).start()

    pl.semaphore_wait(barrier, len(partners))

    def pipeline(s_exp, t_exp):
        def step(t, carry):
            def at_lag(lag, work):
                c = t - lag

                @pl.when((c >= 0) & (c < chunks))
                def _():
                    work(c)

            at_lag(0, functools.partial(statistics, s_exp, t_exp))
            at_lag(2, gradient_over_z)
            at_lag(1, functools.partial(gradient, s_exp, t_exp))
            at_lag(0, statistics_over_z)
            at_lag(3, finish)
            at_lag(4, spread_z)
            at_lag(5, spread_x)
            return carry

        lax.fori_loop(0, chunks + 5, step, 0)

    pl.run_scoped(
        pipeline,
        pltpu.VMEM((2, protos, rows), F32),
        pltpu.VMEM((2, protos, rows), F32),
    )
    for d in range(1, ndp):
        loss_copy(d).start()

    def drain(c, carry):
        for d in range(1, nx):
            all_x_copy(c, d).wait_recv()
            stat_x_copy(c, d).wait_send()
            grad_x_copy(c, d).wait_send()
            all_x_copy(c, d).wait_send()
        for d in range(1, nz):
            stat_z_copy(c, d).wait_send()
            grad_z_copy(c, d).wait_send()
            all_z_copy(c, d).wait_send()
        for d in range(1, ndp):
            dp_copy(c, d).wait_send()
        return carry

    lax.fori_loop(0, chunks, drain, 0)
    for d in range(1, ndp):
        loss_copy(d).wait()


def place_kernel(dims, gathered, losses, counts_ref, row_loss, grad):
    ndp, nz, nx, images, slots, tile = dims
    chunks = images // nx
    piece = slots // nz
    per_res = piece // ndp
    total_images = counts_ref.shape[1]
    me = lax.axis_index("dp")
    counts = counts_ref[...].astype(F32)
    upto = (iota((total_images, total_images), 0) <= iota((total_images, total_images), 1))
    ends = jnp.dot(
        jnp.broadcast_to(counts, (8, total_images)).astype(BF16), upto.astype(F32).astype(BF16),
        preferred_element_type=F32,
    )[0:1, :]
    starts = (ends - counts).astype(jnp.int32)
    ends = ends.astype(jnp.int32)
    b = pl.program_id(0) * tile + iota((tile, 1), 0)
    g = b * ndp + me
    image = jnp.sum((g >= ends).astype(F32), axis=1, keepdims=True).astype(jnp.int32)
    start = jnp.max(jnp.where(g >= starts, starts, 0).astype(F32), axis=1, keepdims=True)
    j = g - start.astype(jnp.int32)
    owner, own_image = image // images, image % images
    at = ((own_image % nx) * chunks + own_image // nx) * nz + j // piece
    at = at * piece + owner * per_res + (j % piece) // ndp
    held = gathered.shape[0]
    pick = (iota((tile, held), 1) == at).astype(F32).astype(BF16)
    grad[...] = jnp.dot(pick, gathered[...], preferred_element_type=F32).astype(BF16)
    wide = losses[...]
    high = wide.astype(BF16)
    rest = wide - high.astype(F32)
    middle = rest.astype(BF16)
    low = (rest - middle.astype(F32)).astype(BF16)
    pick_image = (iota((tile, total_images), 1) == image).astype(F32).astype(BF16)
    lines = sum(
        jnp.dot(pick_image, part, preferred_element_type=F32) for part in (low, middle, high)
    )
    lines = jnp.where(iota((tile, slots), 1) == j, lines, 0.0)
    row_loss[...] = jnp.sum(jnp.transpose(lines), axis=0, keepdims=True)


def local(ndp, nz, nx, student_rows, teacher_rows, student_proto, teacher_proto, center, counts, order):
    images, patches, width = student_rows.shape
    slots = patches // 2
    protos = student_proto.shape[1]
    chunks = images // nx
    rows = nx * slots
    piece = slots // nz
    slot_rows = max(8, piece // ndp)
    block = min(512, protos)
    mask_dev = counts.shape[0] * 96 // ndp
    dims = (ndp, nz, nx, images, slots, block)
    any_spec = pl.BlockSpec(memory_space=pl.ANY)
    vmem = pl.BlockSpec(memory_space=pltpu.VMEM)
    counts = counts[None, :]
    dma = pltpu.SemaphoreType.DMA
    gathered, losses = pl.pallas_call(
        functools.partial(head_kernel, dims),
        out_shape=(
            jax.ShapeDtypeStruct((nx, chunks, nz, piece, width), BF16),
            jax.ShapeDtypeStruct((ndp, images, slots), F32),
        ),
        in_specs=[any_spec] * 4 + [vmem] * 3,
        out_specs=(vmem, vmem),
        scratch_shapes=[
            pltpu.VMEM((width, protos), BF16),
            pltpu.VMEM((protos, width), BF16),
            pltpu.VMEM((protos, width), BF16),
            pltpu.VMEM((protos, 128), F32),
            pltpu.VMEM((images, slots, width), BF16),
            pltpu.VMEM((images * slots, width), BF16),
            pltpu.VMEM((images * slots, width), BF16),
            pltpu.VMEM((chunks, nx, 4, rows), F32),
            pltpu.VMEM((chunks, nz, 4, rows), F32),
            pltpu.VMEM((chunks, nx, slots, width), F32),
            pltpu.VMEM((chunks, nx, slots, width), F32),
            pltpu.VMEM((chunks, nz, piece, width), F32),
            pltpu.VMEM((chunks, nz, piece, width), F32),
            pltpu.VMEM((chunks, ndp, slot_rows, width), F32),
            pltpu.VMEM((chunks, ndp, slot_rows, width), F32),
            dma((4,)),
            dma((chunks, nx)), dma((chunks, nx)),
            dma((chunks, nz)), dma((chunks, nz)),
            dma((chunks, nx)), dma((chunks, nx)),
            dma((chunks, nz)), dma((chunks, nz)),
            dma((chunks, ndp)), dma((chunks, ndp)),
            dma((chunks, nz)), dma((chunks, nz)),
            dma((chunks, nx)), dma((chunks, nx)),
            dma((ndp,)), dma((ndp,)),
        ],
        compiler_params=pltpu.CompilerParams(
            collective_id=0, has_side_effects=True, vmem_limit_bytes=63 * 2**20
        ),
        name="proto_head",
    )(student_rows, teacher_rows, student_proto, teacher_proto, center[None, :], counts, order)
    tile = 256 if mask_dev % 256 == 0 else 128
    held = nx * chunks * nz * piece
    row_loss, grad = pl.pallas_call(
        functools.partial(place_kernel, (ndp, nz, nx, images, slots, tile)),
        grid=(mask_dev // tile,),
        out_shape=(
            jax.ShapeDtypeStruct((1, mask_dev), F32),
            jax.ShapeDtypeStruct((mask_dev, width), BF16),
        ),
        in_specs=[
            pl.BlockSpec((held, width), lambda i: (0, 0)),
            pl.BlockSpec((ndp * images, slots), lambda i: (0, 0)),
            pl.BlockSpec((1, ndp * images), lambda i: (0, 0)),
        ],
        out_specs=(
            pl.BlockSpec((1, tile), lambda i: (0, i)),
            pl.BlockSpec((tile, width), lambda i: (i, 0)),
        ),
        compiler_params=pltpu.CompilerParams(vmem_limit_bytes=32 * 2**20),
        name="place_rows",
    )(gathered.reshape(held, width), losses.reshape(ndp * images, slots), counts)
    return row_loss, grad[None]


def solution(mesh):
    ndp, proto = mesh.shape["dp"], mesh.shape["proto"]
    nx = X_SIZE
    placed = (
        P("dp", None, None),
        P("dp", None, None),
        P(None, "proto"),
        P(None, "proto"),
        P("proto"),
        P(),
        P("dp", None),
    )
    return jax.shard_map(
        functools.partial(local, ndp, proto // nx, nx),
        mesh=mesh,
        in_specs=placed,
        out_specs=(P("dp", None), P("dp", None, None)),
        check_vma=False,
    )
```

```python
import functools
import math

import jax
import jax.numpy as jnp
from jax import lax
from jax.experimental import pallas as pl
from jax.experimental.pallas import tpu as pltpu
from jax.sharding import PartitionSpec as P

STUDENT_TEMP = 0.1
TEACHER_TEMP = 0.07
EPSILON = 1e-06
LOG2E = math.log2(math.e)
X_SIZE = 4
HALVES = 2
DEPTH = 4
F32 = jnp.float32
BF16 = jnp.bfloat16
MESH = pl.DeviceIdType.MESH
NT = (((1,), (1,)), ((), ()))
TN = (((0,), (0,)), ((), ()))


def iota(shape, dim):
    return lax.broadcasted_iota(jnp.int32, shape, dim)


def head_kernel(dims, *refs):
    ndp, nz, nx, images, slots, block, tile = dims
    (student_hbm, teacher_hbm, sproto_hbm, tproto_hbm, center_ref, counts_ref, order_ref,
     row_loss, grad,
     scols, scols_t, tcols_t, center_b, s_in, s_unit, t_unit, stat_x, stat_z, grad_x, got_x,
     grad_z, got_z, own_dp, got_dp, gathered, losses, row_at,
     load_sem, sx_send, sx_recv, sz_send, sz_recv, gx_send, gx_recv, gz_send, gz_recv,
     dp_send, dp_recv, az_send, az_recv, ax_send, ax_recv, lo_send, lo_recv) = refs
    chunks = images // nx
    units = chunks * HALVES
    half = slots // HALVES
    rows = nx * half
    piece = slots // nz
    unit_piece = half // nz
    per_res = piece // ndp
    slot_rows = own_dp.shape[2]
    protos = scols.shape[1]
    width = scols.shape[0]
    patches = order_ref.shape[1]
    total_images = counts_ref.shape[1]
    mask_dev = grad.shape[0]
    held = nx * nz * piece
    me = lax.axis_index("dp")
    q = lax.axis_index("proto")
    z = q // nx
    x = q % nx

    def along_x(d):
        return (me, z * nx + lax.rem(x + d, nx))

    def along_z(d):
        return (me, lax.rem(z + d, nz) * nx + x)

    def along_dp(d):
        return (lax.rem(me + d, ndp), q)

    barrier = pltpu.get_barrier_semaphore()
    partners = (
        [along_x(d) for d in range(1, nx)]
        + [along_z(d) for d in range(1, nz)]
        + [along_dp(d) for d in range(1, ndp)]
    )
    for partner in partners:
        pl.semaphore_signal(barrier, inc=1, device_id=partner, device_id_type=MESH)

    def prologue(srows, trows, tcols):
        loads = [
            pltpu.make_async_copy(src, dst, load_sem.at[i])
            for i, (src, dst) in enumerate(
                ((student_hbm, srows), (teacher_hbm, trows), (sproto_hbm, scols), (tproto_hbm, tcols))
            )
        ]
        for load in loads:
            load.start()

        def spread_center(n, carry):
            for i in range(256 // 128):
                at = pl.ds(pl.multiple_of(n * 256 + i * 128, 128), 128)
                row = center_ref[:, at] * (LOG2E / TEACHER_TEMP)
                center_b[at, :] = jnp.transpose(jnp.broadcast_to(row, (128, 128)))
            return carry

        def gather_chunk(c, carry):
            for i in range(nx):
                image = c * nx + i
                order = order_ref[pl.ds(image, 1), :][:, :slots]
                pick = (iota((patches, slots), 0) == order).astype(F32).astype(BF16)
                for source, units_ref in ((srows, s_unit), (trows, t_unit)):
                    wide = lax.dot_general(pick, source[image], TN, preferred_element_type=F32)
                    if source is srows:
                        s_in[image] = wide.astype(BF16)
                    norm = jnp.sqrt(jnp.sum(wide * wide, axis=1, keepdims=True) + EPSILON)
                    unit = (wide / norm).reshape(nz, HALVES, unit_piece, width)
                    for h in range(HALVES):
                        units_ref[c * HALVES + h, i] = unit[:, h].reshape(half, width).astype(BF16)
            return carry

        def norm_tiles(n, carry):
            for i in range(group):
                at = pl.ds(pl.multiple_of((n * group + i) * 256, 256), 256)
                for cols, turned in ((scols, scols_t), (tcols, tcols_t)):
                    wide = cols[:, at].astype(F32)
                    scale = 1.0 / jnp.sqrt(jnp.sum(wide * wide, axis=0, keepdims=True) + EPSILON)
                    unit = (wide * scale).astype(BF16)
                    if cols is scols:
                        cols[:, at] = unit
                    turned[at, :] = jnp.transpose(unit)
            return carry

        group = min(4, protos // 256)
        lax.fori_loop(0, protos // 256, spread_center, 0)
        loads[0].wait()
        loads[1].wait()
        lax.fori_loop(0, chunks, gather_chunk, 0)
        loads[2].wait()
        loads[3].wait()
        lax.fori_loop(0, protos // (256 * group), norm_tiles, 0)

    pl.run_scoped(
        prologue,
        pltpu.VMEM((images, patches, width), BF16),
        pltpu.VMEM((images, patches, width), BF16),
        pltpu.VMEM((width, protos), BF16),
    )

    def copy(src, dst, send, recv, device):
        return pltpu.make_async_remote_copy(
            src_ref=src, dst_ref=dst, send_sem=send, recv_sem=recv, device_id=device,
            device_id_type=MESH,
        )

    def stat_x_copy(c, d):
        return copy(stat_x.at[c, 0], stat_x.at[c, d], sx_send.at[c, d], sx_recv.at[c, d], along_x(d))

    def stat_z_copy(c, d):
        return copy(stat_z.at[c, 0], stat_z.at[c, d], sz_send.at[c, d], sz_recv.at[c, d], along_z(d))

    def grad_x_copy(c, d):
        return copy(
            grad_x.at[c, lax.rem(x + d, nx)], got_x.at[c, d], gx_send.at[c, d], gx_recv.at[c, d],
            along_x(d),
        )

    def grad_z_copy(c, d):
        return copy(
            grad_z.at[c, lax.rem(z + d, nz)], got_z.at[c, d], gz_send.at[c, d], gz_recv.at[c, d],
            along_z(d),
        )

    def dp_copy(c, d):
        return copy(
            own_dp.at[c, lax.rem(me + d, ndp)], got_dp.at[c, me], dp_send.at[c, d], dp_recv.at[c, d],
            along_dp(d),
        )

    def all_z_copy(c, d):
        block_ref = gathered.at[c, x, z]
        return copy(block_ref, block_ref, az_send.at[c, d], az_recv.at[c, d], along_z(d))

    def all_x_copy(c, d):
        block_ref = gathered.at[c, x]
        return copy(block_ref, block_ref, ax_send.at[c, d], ax_recv.at[c, d], along_x(d))

    def loss_copy(d):
        return copy(losses.at[me], losses.at[me], lo_send.at[d], lo_recv.at[d], along_dp(d))

    def statistics(s_exp, t_exp, c):
        slot = lax.rem(c, DEPTH)
        student = s_unit[c].reshape(rows, width)
        teacher = t_unit[c].reshape(rows, width)
        sums = [jnp.zeros((8, rows), F32)] * 3
        for n in range(0, protos, block):
            at = pl.ds(n, block)
            s = lax.dot_general(scols_t[at, :], student, NT, preferred_element_type=F32)
            t = lax.dot_general(tcols_t[at, :], teacher, NT, preferred_element_type=F32)
            shift = jnp.concatenate([center_b[at, :]] * (rows // 128), axis=1)
            es = jnp.exp2(s * (LOG2E / STUDENT_TEMP))
            et = jnp.exp2(t * (LOG2E / TEACHER_TEMP) - shift)
            s_exp[slot, at, :] = es
            t_exp[slot, at, :] = et
            sums = [
                total + jnp.sum(part.reshape(block // 8, 8, rows), axis=0)
                for total, part in zip(sums, (es, et, et * s))
            ]
        lines = [jnp.sum(total, axis=0, keepdims=True) for total in sums]
        stat_x[c, 0] = jnp.concatenate(lines + [jnp.zeros((1, rows), F32)], axis=0)
        for d in range(1, nx):
            stat_x_copy(c, d).start()

    def statistics_over_z(c):
        total = stat_x[c, 0]
        for d in range(1, nx):
            stat_x_copy(c, d).wait_recv()
            total = total + stat_x[c, d]
        stat_z[c, 0] = total
        for d in range(1, nz):
            stat_z_copy(c, d).start()

    def gradient(s_exp, t_exp, c):
        slot = lax.rem(c, DEPTH)
        total = stat_z[c, 0]
        for d in range(1, nz):
            stat_z_copy(c, d).wait_recv()
            total = total + stat_z[c, d]
        s_sum, t_sum, cross = total[0:1, :], total[1:2, :], total[2:3, :]
        loss = jnp.log(s_sum) - cross * (1.0 / STUDENT_TEMP) / t_sum
        losses[me, pl.ds(c, 1), :] = loss
        s_scale = (1.0 / STUDENT_TEMP) / s_sum
        t_scale = (1.0 / STUDENT_TEMP) / t_sum
        dz = jnp.zeros((width, rows), F32)
        for n in range(0, protos, block):
            at = pl.ds(n, block)
            dlogit = (s_exp[slot, at, :] * s_scale - t_exp[slot, at, :] * t_scale).astype(BF16)
            dz = dz + jnp.dot(scols[:, at], dlogit, preferred_element_type=F32)
        grad_x[c] = jnp.transpose(dz).reshape(nx, half, width)
        for d in range(1, nx):
            grad_x_copy(c, d).start()

    def gradient_over_z(c):
        total = grad_x[c, x]
        for d in range(1, nx):
            grad_x_copy(c, d).wait_recv()
            total = total + got_x[c, d]
        grad_z[c] = total.reshape(nz, unit_piece, width)
        for d in range(1, nz):
            grad_z_copy(c, d).start()

    def finish(c):
        parts = []
        for h in range(HALVES):
            u = c * HALVES + h
            part = grad_z[u, z]
            for d in range(1, nz):
                grad_z_copy(u, d).wait_recv()
                part = part + got_z[u, d]
            parts.append(part)
        dz = jnp.concatenate(parts, axis=0)
        image = c * nx + x
        xs = s_in[image, pl.ds(pl.multiple_of(z * piece, piece), piece), :].astype(F32)
        norm = jnp.sqrt(jnp.sum(xs * xs, axis=1, keepdims=True) + EPSILON)
        inner = jnp.sum(xs * dz, axis=1, keepdims=True)
        dx = (dz / norm - xs * inner / (norm * norm * norm)).astype(BF16)
        before = iota(counts_ref.shape, 1) < me * images + image
        start = jnp.sum(jnp.where(before, counts_ref[...].astype(F32), 0.0), axis=1, keepdims=True)
        first = jnp.broadcast_to(start.astype(jnp.int32), (ndp * slot_rows, piece))
        pos = iota((ndp * slot_rows, piece), 0)
        k = iota((ndp * slot_rows, piece), 1)
        pick = (((first + k) % ndp) == pos // slot_rows) & (k // ndp == pos % slot_rows)
        sent = jnp.dot(pick.astype(F32).astype(BF16), dx, preferred_element_type=F32)
        own_dp[c] = sent.reshape(ndp, slot_rows, width)
        for d in range(1, ndp):
            dp_copy(c, d).start()
        got_dp[c, me] = own_dp[c, me]

    def spread_z(c):
        for d in range(1, ndp):
            dp_copy(c, d).wait_recv()
        held = got_dp[c].reshape(ndp * slot_rows, width).astype(BF16)
        pos = iota((piece, ndp * slot_rows), 0)
        k = iota((piece, ndp * slot_rows), 1)
        pick = (k // slot_rows == pos // per_res) & (k % slot_rows == pos % per_res)
        gathered[c, x, z] = jnp.dot(
            pick.astype(F32).astype(BF16), held, preferred_element_type=F32
        ).astype(BF16)
        for d in range(1, nz):
            all_z_copy(c, d).start()

    def spread_x(c):
        for d in range(1, nz):
            all_z_copy(c, d).wait_recv()
        for d in range(1, nx):
            all_x_copy(c, d).start()

    def row_of(n):
        counts = counts_ref[...].astype(F32)
        upto = iota((total_images, total_images), 0) <= iota((total_images, total_images), 1)
        ends = jnp.dot(
            jnp.broadcast_to(counts, (8, total_images)).astype(BF16),
            upto.astype(F32).astype(BF16), preferred_element_type=F32,
        )[0:1, :]
        starts = ends - counts
        g = (n * tile + iota((tile, 1), 0)) * ndp + me
        wide = g.astype(F32)
        image = jnp.sum((wide >= ends).astype(F32), axis=1, keepdims=True).astype(jnp.int32)
        start = jnp.max(jnp.where(wide >= starts, starts, 0.0), axis=1, keepdims=True)
        return image // images, image % images, g - start.astype(jnp.int32)

    def index_rows():
        for n in range(mask_dev // tile):
            owner, image, j = row_of(n)
            at = image * nz + j // piece
            at = at * piece + owner * per_res + (j % piece) // ndp
            row_at[n * tile : (n + 1) * tile, :] = jnp.broadcast_to(at, (tile, 128))
        grad[...] = jnp.zeros_like(grad)

    def place(c):
        for d in range(1, nx):
            all_x_copy(c, d).wait_recv()
        values = gathered[c].reshape(held, width)
        for n in range(mask_dev // tile):
            at = jnp.concatenate([row_at[n * tile : (n + 1) * tile, :]] * (held // 128), axis=1)
            pick = (iota((tile, held), 1) + c * held == at).astype(F32).astype(BF16)
            put = jnp.dot(pick, values, preferred_element_type=F32)
            lines = slice(n * tile, (n + 1) * tile)
            grad[lines, :] = (grad[lines, :].astype(F32) + put).astype(BF16)

    def send_losses():
        for d in range(1, ndp):
            loss_copy(d).start()

    def place_losses():
        for d in range(1, ndp):
            loss_copy(d).wait_recv()
        wide = losses[...].reshape(ndp * units, rows)
        high = wide.astype(BF16)
        rest = wide - high.astype(F32)
        middle = rest.astype(BF16)
        low = (rest - middle.astype(F32)).astype(BF16)
        for n in range(mask_dev // tile):
            owner, image, j = row_of(n)
            line = owner * units + (image // nx) * HALVES + (j // unit_piece) % HALVES
            lane = (image % nx) * half + (j // piece) * unit_piece + j % unit_piece
            pick = (iota((tile, ndp * units), 1) == line).astype(F32).astype(BF16)
            lines = sum(
                jnp.dot(pick, part, preferred_element_type=F32) for part in (low, middle, high)
            )
            lines = jnp.where(iota((tile, rows), 1) == lane, lines, 0.0)
            row_loss[:, n * tile : (n + 1) * tile] = jnp.sum(
                jnp.transpose(lines), axis=0, keepdims=True
            )

    pl.semaphore_wait(barrier, len(partners))

    def pipeline(s_exp, t_exp):
        def step(t, carry):
            def at_lag(lag, work, every=1):
                u = t - lag

                @pl.when((u >= 0) & (u < units) & (lax.rem(u, every) == every - 1))
                def _():
                    work(u // every)

            at_lag(0, functools.partial(statistics, s_exp, t_exp))
            at_lag(1, statistics_over_z)
            at_lag(DEPTH - 1, functools.partial(gradient, s_exp, t_exp))

            @pl.when(t == units + DEPTH - 2)
            def _():
                send_losses()
                index_rows()

            at_lag(5, gradient_over_z)
            at_lag(6, finish, HALVES)
            at_lag(7, spread_z, HALVES)
            at_lag(8, spread_x, HALVES)

            @pl.when(t == units + DEPTH)
            def _():
                place_losses()

            at_lag(9, place, HALVES)
            return carry

        lax.fori_loop(0, units + 9, step, 0)

    pl.run_scoped(
        pipeline,
        pltpu.VMEM((DEPTH, protos, rows), F32),
        pltpu.VMEM((DEPTH, protos, rows), F32),
    )
    def drain_unit(u, carry):
        for d in range(1, nx):
            stat_x_copy(u, d).wait_send()
            grad_x_copy(u, d).wait_send()
        for d in range(1, nz):
            stat_z_copy(u, d).wait_send()
            grad_z_copy(u, d).wait_send()
        return carry

    def drain_chunk(c, carry):
        for d in range(1, nx):
            all_x_copy(c, d).wait_send()
        for d in range(1, nz):
            all_z_copy(c, d).wait_send()
        for d in range(1, ndp):
            dp_copy(c, d).wait_send()
        return carry

    lax.fori_loop(0, units, drain_unit, 0)
    lax.fori_loop(0, chunks, drain_chunk, 0)
    for d in range(1, ndp):
        loss_copy(d).wait_send()


def local(ndp, nz, nx, student_rows, teacher_rows, student_proto, teacher_proto, center, counts, order):
    images, patches, width = student_rows.shape
    slots = patches // 2
    protos = student_proto.shape[1]
    chunks = images // nx
    units = chunks * HALVES
    half = slots // HALVES
    rows = nx * half
    piece = slots // nz
    slot_rows = max(8, piece // ndp)
    mask_dev = counts.shape[0] * 96 // ndp
    tile = 256 if mask_dev % 256 == 0 else 128
    dims = (ndp, nz, nx, images, slots, min(512, protos), tile)
    any_spec = pl.BlockSpec(memory_space=pl.ANY)
    vmem = pl.BlockSpec(memory_space=pltpu.VMEM)
    dma = pltpu.SemaphoreType.DMA
    row_loss, grad = pl.pallas_call(
        functools.partial(head_kernel, dims),
        out_shape=(
            jax.ShapeDtypeStruct((1, mask_dev), F32),
            jax.ShapeDtypeStruct((mask_dev, width), BF16),
        ),
        in_specs=[any_spec] * 4 + [vmem] * 3,
        out_specs=(vmem, vmem),
        scratch_shapes=[
            pltpu.VMEM((width, protos), BF16),
            pltpu.VMEM((protos, width), BF16),
            pltpu.VMEM((protos, width), BF16),
            pltpu.VMEM((protos, 128), F32),
            pltpu.VMEM((images, slots, width), BF16),
            pltpu.VMEM((units, nx, half, width), BF16),
            pltpu.VMEM((units, nx, half, width), BF16),
            pltpu.VMEM((units, nx, 4, rows), F32),
            pltpu.VMEM((units, nz, 4, rows), F32),
            pltpu.VMEM((units, nx, half, width), F32),
            pltpu.VMEM((units, nx, half, width), F32),
            pltpu.VMEM((units, nz, half // nz, width), F32),
            pltpu.VMEM((units, nz, half // nz, width), F32),
            pltpu.VMEM((chunks, ndp, slot_rows, width), F32),
            pltpu.VMEM((chunks, ndp, slot_rows, width), F32),
            pltpu.VMEM((chunks, nx, nz, piece, width), BF16),
            pltpu.VMEM((ndp, units, rows), F32),
            pltpu.VMEM((mask_dev, 128), jnp.int32),
            dma((4,)),
            dma((units, nx)), dma((units, nx)),
            dma((units, nz)), dma((units, nz)),
            dma((units, nx)), dma((units, nx)),
            dma((units, nz)), dma((units, nz)),
            dma((chunks, ndp)), dma((chunks, ndp)),
            dma((chunks, nz)), dma((chunks, nz)),
            dma((chunks, nx)), dma((chunks, nx)),
            dma((ndp,)), dma((ndp,)),
        ],
        compiler_params=pltpu.CompilerParams(
            collective_id=0, has_side_effects=True, vmem_limit_bytes=63 * 2**20
        ),
        name="proto_head",
    )(student_rows, teacher_rows, student_proto, teacher_proto, center[None, :], counts[None, :], order)
    return row_loss, grad[None]


def solution(mesh):
    ndp, proto = mesh.shape["dp"], mesh.shape["proto"]
    nx = X_SIZE
    placed = (
        P("dp", None, None),
        P("dp", None, None),
        P(None, "proto"),
        P(None, "proto"),
        P("proto"),
        P(),
        P("dp", None),
    )
    return jax.shard_map(
        functools.partial(local, ndp, proto // nx, nx),
        mesh=mesh,
        in_specs=placed,
        out_specs=(P("dp", None), P("dp", None, None)),
        check_vma=False,
    )
```

```python
import functools
import math

import jax
import jax.numpy as jnp
from jax import lax
from jax.experimental import pallas as pl
from jax.experimental.pallas import tpu as pltpu
from jax.sharding import PartitionSpec as P

STUDENT_TEMP = 0.1
TEACHER_TEMP = 0.07
EPSILON = 1e-06
LOG2E = math.log2(math.e)
X_SIZE = 4
HALVES = 2
DEPTH = 4
F32 = jnp.float32
BF16 = jnp.bfloat16
MESH = pl.DeviceIdType.MESH
NT = (((1,), (1,)), ((), ()))
TN = (((0,), (0,)), ((), ()))


def iota(shape, dim):
    return lax.broadcasted_iota(jnp.int32, shape, dim)


def head_kernel(dims, *refs):
    ndp, nz, nx, images, slots, block, tile = dims
    (student_hbm, teacher_hbm, sproto_hbm, tproto_hbm, center_ref, counts_ref, order_ref,
     row_loss, grad,
     scols, scols_t, tcols_t, center_b, s_in, s_unit, t_unit, stat_x, stat_z, grad_x, got_x,
     grad_z, got_z, own_dp, got_dp, gathered, losses, row_at, row_key,
     load_sem, sx_send, sx_recv, sz_send, sz_recv, gx_send, gx_recv, gz_send, gz_recv,
     dp_send, dp_recv, az_send, az_recv, ax_send, ax_recv, lo_send, lo_recv) = refs
    chunks = images // nx
    units = chunks * HALVES
    half = slots // HALVES
    rows = nx * half
    piece = slots // nz
    unit_piece = half // nz
    per_res = piece // ndp
    slot_rows = own_dp.shape[2]
    protos = scols.shape[1]
    width = scols.shape[0]
    patches = order_ref.shape[1]
    total_images = counts_ref.shape[1]
    mask_dev = grad.shape[0]
    held = nx * nz * piece
    me = lax.axis_index("dp")
    q = lax.axis_index("proto")
    z = q // nx
    x = q % nx

    def along_x(d):
        return (me, z * nx + lax.rem(x + d, nx))

    def along_z(d):
        return (me, lax.rem(z + d, nz) * nx + x)

    def along_dp(d):
        return (lax.rem(me + d, ndp), q)

    barrier = pltpu.get_barrier_semaphore()
    partners = (
        [along_x(d) for d in range(1, nx)]
        + [along_z(d) for d in range(1, nz)]
        + [along_dp(d) for d in range(1, ndp)]
    )
    for partner in partners:
        pl.semaphore_signal(barrier, inc=1, device_id=partner, device_id_type=MESH)

    def prologue(srows, trows, tcols):
        loads = [
            pltpu.make_async_copy(src, dst, load_sem.at[i])
            for i, (src, dst) in enumerate(
                ((student_hbm, srows), (teacher_hbm, trows), (sproto_hbm, scols), (tproto_hbm, tcols))
            )
        ]
        for load in loads:
            load.start()

        def spread_center(n, carry):
            for i in range(256 // 128):
                at = pl.ds(pl.multiple_of(n * 256 + i * 128, 128), 128)
                row = center_ref[:, at] * (LOG2E / TEACHER_TEMP)
                center_b[at, :] = jnp.transpose(jnp.broadcast_to(row, (128, 128)))
            return carry

        def gather_chunk(c, carry):
            for i in range(nx):
                image = c * nx + i
                order = order_ref[pl.ds(image, 1), :][:, :slots]
                pick = (iota((patches, slots), 0) == order).astype(F32).astype(BF16)
                for source, units_ref in ((srows, s_unit), (trows, t_unit)):
                    wide = lax.dot_general(pick, source[image], TN, preferred_element_type=F32)
                    if source is srows:
                        s_in[image] = wide.astype(BF16)
                    norm = jnp.sqrt(jnp.sum(wide * wide, axis=1, keepdims=True) + EPSILON)
                    unit = (wide / norm).reshape(nz, HALVES, unit_piece, width)
                    for h in range(HALVES):
                        units_ref[c * HALVES + h, i] = unit[:, h].reshape(half, width).astype(BF16)
            return carry

        def norm_tiles(n, carry):
            for i in range(group):
                at = pl.ds(pl.multiple_of((n * group + i) * 256, 256), 256)
                for cols, turned in ((scols, scols_t), (tcols, tcols_t)):
                    wide = cols[:, at].astype(F32)
                    scale = 1.0 / jnp.sqrt(jnp.sum(wide * wide, axis=0, keepdims=True) + EPSILON)
                    unit = (wide * scale).astype(BF16)
                    if cols is scols:
                        cols[:, at] = unit
                    turned[at, :] = jnp.transpose(unit)
            return carry

        group = protos // 256 // chunks

        def prepare(c, carry):
            gather_chunk(c, carry)
            return norm_tiles(c, carry)

        lax.fori_loop(0, protos // 256, spread_center, 0)
        for load in loads:
            load.wait()
        lax.fori_loop(0, chunks, prepare, 0)

    pl.run_scoped(
        prologue,
        pltpu.VMEM((images, patches, width), BF16),
        pltpu.VMEM((images, patches, width), BF16),
        pltpu.VMEM((width, protos), BF16),
    )

    def copy(src, dst, send, recv, device):
        return pltpu.make_async_remote_copy(
            src_ref=src, dst_ref=dst, send_sem=send, recv_sem=recv, device_id=device,
            device_id_type=MESH,
        )

    def stat_x_copy(c, d):
        return copy(stat_x.at[c, 0], stat_x.at[c, d], sx_send.at[c, d], sx_recv.at[c, d], along_x(d))

    def stat_z_copy(c, d):
        return copy(stat_z.at[c, 0], stat_z.at[c, d], sz_send.at[c, d], sz_recv.at[c, d], along_z(d))

    def grad_x_copy(c, d):
        return copy(
            grad_x.at[c, lax.rem(x + d, nx)], got_x.at[c, d], gx_send.at[c, d], gx_recv.at[c, d],
            along_x(d),
        )

    def grad_z_copy(c, d):
        return copy(
            grad_z.at[c, lax.rem(z + d, nz)], got_z.at[c, d], gz_send.at[c, d], gz_recv.at[c, d],
            along_z(d),
        )

    def dp_copy(c, d):
        return copy(
            own_dp.at[c, lax.rem(me + d, ndp)], got_dp.at[c, me], dp_send.at[c, d], dp_recv.at[c, d],
            along_dp(d),
        )

    def all_z_copy(c, d):
        block_ref = gathered.at[c, x, z]
        return copy(block_ref, block_ref, az_send.at[c, d], az_recv.at[c, d], along_z(d))

    def all_x_copy(c, d):
        block_ref = gathered.at[c, x]
        return copy(block_ref, block_ref, ax_send.at[c, d], ax_recv.at[c, d], along_x(d))

    def loss_copy(d):
        return copy(losses.at[me], losses.at[me], lo_send.at[d], lo_recv.at[d], along_dp(d))

    def statistics(s_exp, t_exp, c):
        slot = lax.rem(c, DEPTH)
        student = s_unit[c].reshape(rows, width)
        teacher = t_unit[c].reshape(rows, width)
        sums = [jnp.zeros((8, rows), F32)] * 3
        for n in range(0, protos, block):
            at = pl.ds(n, block)
            s = lax.dot_general(scols_t[at, :], student, NT, preferred_element_type=F32)
            t = lax.dot_general(tcols_t[at, :], teacher, NT, preferred_element_type=F32)
            shift = jnp.concatenate([center_b[at, :]] * (rows // 128), axis=1)
            es = jnp.exp2(s * (LOG2E / STUDENT_TEMP))
            et = jnp.exp2(t * (LOG2E / TEACHER_TEMP) - shift)
            s_exp[slot, at, :] = es
            t_exp[slot, at, :] = et
            sums = [
                total + jnp.sum(part.reshape(block // 8, 8, rows), axis=0)
                for total, part in zip(sums, (es, et, et * s))
            ]
        lines = [jnp.sum(total, axis=0, keepdims=True) for total in sums]
        stat_x[c, 0] = jnp.concatenate(lines + [jnp.zeros((1, rows), F32)], axis=0)
        for d in range(1, nx):
            stat_x_copy(c, d).start()

    def statistics_over_z(c):
        total = stat_x[c, 0]
        for d in range(1, nx):
            stat_x_copy(c, d).wait_recv()
            total = total + stat_x[c, d]
        stat_z[c, 0] = total
        for d in range(1, nz):
            stat_z_copy(c, d).start()

    def gradient(s_exp, t_exp, c):
        slot = lax.rem(c, DEPTH)
        total = stat_z[c, 0]
        for d in range(1, nz):
            stat_z_copy(c, d).wait_recv()
            total = total + stat_z[c, d]
        s_sum, t_sum, cross = total[0:1, :], total[1:2, :], total[2:3, :]
        loss = jnp.log(s_sum) - cross * (1.0 / STUDENT_TEMP) / t_sum
        losses[me, pl.ds(c, 1), :] = loss
        s_scale = (1.0 / STUDENT_TEMP) / s_sum
        t_scale = (1.0 / STUDENT_TEMP) / t_sum
        dz = jnp.zeros((width, rows), F32)
        for n in range(0, protos, block):
            at = pl.ds(n, block)
            dlogit = (s_exp[slot, at, :] * s_scale - t_exp[slot, at, :] * t_scale).astype(BF16)
            dz = dz + jnp.dot(scols[:, at], dlogit, preferred_element_type=F32)
        grad_x[c] = jnp.transpose(dz).reshape(nx, half, width)
        for d in range(1, nx):
            grad_x_copy(c, d).start()

    def gradient_over_z(c):
        total = grad_x[c, x]
        for d in range(1, nx):
            grad_x_copy(c, d).wait_recv()
            total = total + got_x[c, d]
        grad_z[c] = total.reshape(nz, unit_piece, width)
        for d in range(1, nz):
            grad_z_copy(c, d).start()

    def finish(c):
        parts = []
        for h in range(HALVES):
            u = c * HALVES + h
            part = grad_z[u, z]
            for d in range(1, nz):
                grad_z_copy(u, d).wait_recv()
                part = part + got_z[u, d]
            parts.append(part)
        dz = jnp.concatenate(parts, axis=0)
        image = c * nx + x
        xs = s_in[image, pl.ds(pl.multiple_of(z * piece, piece), piece), :].astype(F32)
        norm = jnp.sqrt(jnp.sum(xs * xs, axis=1, keepdims=True) + EPSILON)
        inner = jnp.sum(xs * dz, axis=1, keepdims=True)
        dx = (dz / norm - xs * inner / (norm * norm * norm)).astype(BF16)
        before = iota(counts_ref.shape, 1) < me * images + image
        start = jnp.sum(jnp.where(before, counts_ref[...].astype(F32), 0.0), axis=1, keepdims=True)
        first = jnp.broadcast_to(start.astype(jnp.int32), (ndp * slot_rows, piece))
        pos = iota((ndp * slot_rows, piece), 0)
        k = iota((ndp * slot_rows, piece), 1)
        pick = (((first + k) % ndp) == pos // slot_rows) & (k // ndp == pos % slot_rows)
        sent = jnp.dot(pick.astype(F32).astype(BF16), dx, preferred_element_type=F32)
        own_dp[c] = sent.reshape(ndp, slot_rows, width)
        for d in range(1, ndp):
            dp_copy(c, d).start()
        got_dp[c, me] = own_dp[c, me]

    def spread_z(c):
        for d in range(1, ndp):
            dp_copy(c, d).wait_recv()
        held = got_dp[c].reshape(ndp * slot_rows, width).astype(BF16)
        pos = iota((piece, ndp * slot_rows), 0)
        k = iota((piece, ndp * slot_rows), 1)
        pick = (k // slot_rows == pos // per_res) & (k % slot_rows == pos % per_res)
        gathered[c, x, z] = jnp.dot(
            pick.astype(F32).astype(BF16), held, preferred_element_type=F32
        ).astype(BF16)
        for d in range(1, nz):
            all_z_copy(c, d).start()

    def spread_x(c):
        for d in range(1, nz):
            all_z_copy(c, d).wait_recv()
        for d in range(1, nx):
            all_x_copy(c, d).start()

    def index_rows():
        counts = counts_ref[...].astype(F32)
        upto = iota((total_images, total_images), 0) <= iota((total_images, total_images), 1)
        ends = jnp.dot(
            jnp.broadcast_to(counts, (8, total_images)).astype(BF16),
            upto.astype(F32).astype(BF16), preferred_element_type=F32,
        )[0:1, :]
        starts = ends - counts

        def index_tile(n, carry):
            g = (n * tile + iota((tile, 1), 0)) * ndp + me
            wide = g.astype(F32)
            image = jnp.sum((wide >= ends).astype(F32), axis=1, keepdims=True).astype(jnp.int32)
            start = jnp.max(jnp.where(wide >= starts, starts, 0.0), axis=1, keepdims=True)
            j = g - start.astype(jnp.int32)
            owner, image = image // images, image % images
            at = (image * nz + j // piece) * piece + owner * per_res + (j % piece) // ndp
            lines = pl.ds(pl.multiple_of(n * tile, tile), tile)
            row_at[lines, :] = jnp.broadcast_to(at, (tile, 128))
            line = owner * units + (image // nx) * HALVES + (j // unit_piece) % HALVES
            lane = (image % nx) * half + (j // piece) * unit_piece + j % unit_piece
            row_key[lines, :] = jnp.broadcast_to(line * rows + lane, (tile, 128))
            return carry

        lax.fori_loop(0, mask_dev // tile, index_tile, 0)
        grad[...] = jnp.zeros_like(grad)

    def place(c):
        for d in range(1, nx):
            all_x_copy(c, d).wait_recv()
        values = gathered[c].reshape(held, width)

        def place_tile(n, carry):
            lines = pl.ds(pl.multiple_of(n * tile, tile), tile)
            at = jnp.concatenate([row_at[lines, :] - c * held] * (held // 128), axis=1)
            pick = (iota((tile, held), 1) == at).astype(F32).astype(BF16)
            put = jnp.dot(pick, values, preferred_element_type=F32)
            grad[lines, :] = (grad[lines, :].astype(F32) + put).astype(BF16)
            return carry

        lax.fori_loop(0, mask_dev // tile, place_tile, 0)

    def send_losses():
        for d in range(1, ndp):
            loss_copy(d).start()

    def place_losses():
        for d in range(1, ndp):
            loss_copy(d).wait_recv()
        wide = losses[...].reshape(ndp * units, rows)
        high = wide.astype(BF16)
        rest = wide - high.astype(F32)
        middle = rest.astype(BF16)
        low = (rest - middle.astype(F32)).astype(BF16)

        for n in range(mask_dev // tile):
            key = row_key[n * tile : (n + 1) * tile, :]
            line, lane = key // rows, key % rows
            pick = (iota((tile, 128), 1) == line).astype(F32).astype(BF16)[:, : ndp * units]
            lines = sum(
                jnp.dot(pick, part, preferred_element_type=F32) for part in (low, middle, high)
            )
            lane = jnp.concatenate([lane] * (rows // 128), axis=1)
            lines = jnp.where(iota((tile, rows), 1) == lane, lines, 0.0)
            row_loss[:, n * tile : (n + 1) * tile] = jnp.sum(
                jnp.transpose(lines), axis=0, keepdims=True
            )

    pl.semaphore_wait(barrier, len(partners))

    def pipeline(s_exp, t_exp):
        def step(t, carry):
            def at_lag(lag, work, every=1):
                u = t - lag

                @pl.when((u >= 0) & (u < units) & (lax.rem(u, every) == every - 1))
                def _():
                    work(u // every)

            @pl.when(t == DEPTH)
            def _():
                index_rows()

            at_lag(DEPTH, functools.partial(gradient, s_exp, t_exp))
            at_lag(1, statistics_over_z)
            at_lag(0, functools.partial(statistics, s_exp, t_exp))
            at_lag(DEPTH + 2, gradient_over_z)
            at_lag(DEPTH + 3, finish, HALVES)
            at_lag(DEPTH + 4, spread_z, HALVES)
            return carry

        lax.fori_loop(0, units + DEPTH, step, 0)

    pl.run_scoped(
        pipeline,
        pltpu.VMEM((DEPTH, protos, rows), F32),
        pltpu.VMEM((DEPTH, protos, rows), F32),
    )
    def each(first, last, work):
        def one(c, carry):
            work(c)
            return carry

        lax.fori_loop(first, last, one, 0)

    last = chunks - 1
    send_losses()
    finish(last - 1)
    each(units - 2, units, gradient_over_z)
    spread_z(last - 1)
    each(0, last - 1, spread_x)
    finish(last)
    place_losses()
    spread_x(last - 1)
    spread_z(last)
    each(0, last - 1, place)
    spread_x(last)
    each(last - 1, chunks, place)

    def drain_unit(u, carry):
        for d in range(1, nx):
            stat_x_copy(u, d).wait_send()
            grad_x_copy(u, d).wait_send()
        for d in range(1, nz):
            stat_z_copy(u, d).wait_send()
            grad_z_copy(u, d).wait_send()
        return carry

    def drain_chunk(c, carry):
        for d in range(1, nx):
            all_x_copy(c, d).wait_send()
        for d in range(1, nz):
            all_z_copy(c, d).wait_send()
        for d in range(1, ndp):
            dp_copy(c, d).wait_send()
        return carry

    lax.fori_loop(0, units, drain_unit, 0)
    lax.fori_loop(0, chunks, drain_chunk, 0)
    for d in range(1, ndp):
        loss_copy(d).wait_send()


def local(ndp, nz, nx, student_rows, teacher_rows, student_proto, teacher_proto, center, counts, order):
    images, patches, width = student_rows.shape
    slots = patches // 2
    protos = student_proto.shape[1]
    chunks = images // nx
    units = chunks * HALVES
    half = slots // HALVES
    rows = nx * half
    piece = slots // nz
    slot_rows = max(8, piece // ndp)
    mask_dev = counts.shape[0] * 96 // ndp
    tile = 256 if mask_dev % 256 == 0 else 128
    dims = (ndp, nz, nx, images, slots, min(512, protos), tile)
    any_spec = pl.BlockSpec(memory_space=pl.ANY)
    vmem = pl.BlockSpec(memory_space=pltpu.VMEM)
    dma = pltpu.SemaphoreType.DMA
    row_loss, grad = pl.pallas_call(
        functools.partial(head_kernel, dims),
        out_shape=(
            jax.ShapeDtypeStruct((1, mask_dev), F32),
            jax.ShapeDtypeStruct((mask_dev, width), BF16),
        ),
        in_specs=[any_spec] * 4 + [vmem] * 3,
        out_specs=(vmem, vmem),
        scratch_shapes=[
            pltpu.VMEM((width, protos), BF16),
            pltpu.VMEM((protos, width), BF16),
            pltpu.VMEM((protos, width), BF16),
            pltpu.VMEM((protos, 128), F32),
            pltpu.VMEM((images, slots, width), BF16),
            pltpu.VMEM((units, nx, half, width), BF16),
            pltpu.VMEM((units, nx, half, width), BF16),
            pltpu.VMEM((units, nx, 4, rows), F32),
            pltpu.VMEM((units, nz, 4, rows), F32),
            pltpu.VMEM((units, nx, half, width), F32),
            pltpu.VMEM((units, nx, half, width), F32),
            pltpu.VMEM((units, nz, half // nz, width), F32),
            pltpu.VMEM((units, nz, half // nz, width), F32),
            pltpu.VMEM((chunks, ndp, slot_rows, width), F32),
            pltpu.VMEM((chunks, ndp, slot_rows, width), F32),
            pltpu.VMEM((chunks, nx, nz, piece, width), BF16),
            pltpu.VMEM((ndp, units, rows), F32),
            pltpu.VMEM((mask_dev, 128), jnp.int32),
            pltpu.VMEM((mask_dev, 128), jnp.int32),
            dma((4,)),
            dma((units, nx)), dma((units, nx)),
            dma((units, nz)), dma((units, nz)),
            dma((units, nx)), dma((units, nx)),
            dma((units, nz)), dma((units, nz)),
            dma((chunks, ndp)), dma((chunks, ndp)),
            dma((chunks, nz)), dma((chunks, nz)),
            dma((chunks, nx)), dma((chunks, nx)),
            dma((ndp,)), dma((ndp,)),
        ],
        compiler_params=pltpu.CompilerParams(
            collective_id=0, has_side_effects=True, vmem_limit_bytes=63 * 2**20
        ),
        name="proto_head",
    )(student_rows, teacher_rows, student_proto, teacher_proto, center[None, :], counts[None, :], order)
    return row_loss, grad[None]


def solution(mesh):
    ndp, proto = mesh.shape["dp"], mesh.shape["proto"]
    nx = X_SIZE
    placed = (
        P("dp", None, None),
        P("dp", None, None),
        P(None, "proto"),
        P(None, "proto"),
        P("proto"),
        P(),
        P("dp", None),
    )
    return jax.shard_map(
        functools.partial(local, ndp, proto // nx, nx),
        mesh=mesh,
        in_specs=placed,
        out_specs=(P("dp", None), P("dp", None, None)),
        check_vma=False,
    )
```

```python
import functools
import math

import jax
import jax.numpy as jnp
from jax import lax
from jax.experimental import pallas as pl
from jax.experimental.pallas import tpu as pltpu
from jax.sharding import PartitionSpec as P

STUDENT_TEMP = 0.1
TEACHER_TEMP = 0.07
EPSILON = 1e-06
LOG2E = math.log2(math.e)
X_SIZE = 4
HALVES = 2
DEPTH = 4
F32 = jnp.float32
BF16 = jnp.bfloat16
MESH = pl.DeviceIdType.MESH
NT = (((1,), (1,)), ((), ()))
TN = (((0,), (0,)), ((), ()))


def iota(shape, dim):
    return lax.broadcasted_iota(jnp.int32, shape, dim)


def head_kernel(dims, *refs):
    ndp, nz, nx, images, slots, block, tile = dims
    (student_hbm, teacher_hbm, sproto_hbm, tproto_hbm, center_ref, counts_ref, order_ref,
     row_loss, grad,
     scols, scols_t, tcols_t, center_b, s_in, s_unit, t_unit, stat_x, stat_z, grad_x, got_x,
     grad_z, got_z, own_dp, got_dp, gathered, losses, row_at, row_key,
     load_sem, sx_send, sx_recv, sz_send, sz_recv, gx_send, gx_recv, gz_send, gz_recv,
     dp_send, dp_recv, az_send, az_recv, ax_send, ax_recv, lo_send, lo_recv) = refs
    chunks = images // nx
    units = chunks * HALVES
    half = slots // HALVES
    rows = nx * half
    piece = slots // nz
    unit_piece = half // nz
    per_res = piece // ndp
    slot_rows = own_dp.shape[2]
    protos = scols.shape[1]
    width = scols.shape[0]
    patches = order_ref.shape[1]
    total_images = counts_ref.shape[1]
    mask_dev = grad.shape[0]
    held = nx * nz * piece
    me = lax.axis_index("dp")
    q = lax.axis_index("proto")
    z = q // nx
    x = q % nx

    def along_x(d):
        return (me, z * nx + lax.rem(x + d, nx))

    def along_z(d):
        return (me, lax.rem(z + d, nz) * nx + x)

    def along_dp(d):
        return (lax.rem(me + d, ndp), q)

    barrier = pltpu.get_barrier_semaphore()
    partners = (
        [along_x(d) for d in range(1, nx)]
        + [along_z(d) for d in range(1, nz)]
        + [along_dp(d) for d in range(1, ndp)]
    )
    for partner in partners:
        pl.semaphore_signal(barrier, inc=1, device_id=partner, device_id_type=MESH)

    def prologue(srows, trows, tcols):
        loads = [
            pltpu.make_async_copy(src, dst, load_sem.at[i])
            for i, (src, dst) in enumerate(
                ((student_hbm, srows), (teacher_hbm, trows), (sproto_hbm, scols), (tproto_hbm, tcols))
            )
        ]
        for load in loads:
            load.start()

        def spread_center(n, carry):
            for i in range(256 // 128):
                at = pl.ds(pl.multiple_of(n * 256 + i * 128, 128), 128)
                row = center_ref[:, at] * (LOG2E / TEACHER_TEMP)
                center_b[at, :] = jnp.transpose(jnp.broadcast_to(row, (128, 128)))
            return carry

        def gather_chunk(c, carry):
            for i in range(nx):
                image = c * nx + i
                order = order_ref[pl.ds(image, 1), :][:, :slots]
                pick = (iota((patches, slots), 0) == order).astype(F32).astype(BF16)
                for source, units_ref in ((srows, s_unit), (trows, t_unit)):
                    wide = lax.dot_general(pick, source[image], TN, preferred_element_type=F32)
                    if source is srows:
                        s_in[image] = wide.astype(BF16)
                    norm = jnp.sqrt(jnp.sum(wide * wide, axis=1, keepdims=True) + EPSILON)
                    unit = (wide / norm).reshape(nz, HALVES, unit_piece, width)
                    for h in range(HALVES):
                        units_ref[c * HALVES + h, i] = unit[:, h].reshape(half, width).astype(BF16)
            return carry

        def norm_tiles(n, carry):
            for i in range(group):
                at = pl.ds(pl.multiple_of((n * group + i) * 256, 256), 256)
                for cols, turned in ((scols, scols_t), (tcols, tcols_t)):
                    wide = cols[:, at].astype(F32)
                    scale = 1.0 / jnp.sqrt(jnp.sum(wide * wide, axis=0, keepdims=True) + EPSILON)
                    unit = (wide * scale).astype(BF16)
                    if cols is scols:
                        cols[:, at] = unit
                    turned[at, :] = jnp.transpose(unit)
            return carry

        group = protos // 256 // chunks

        def prepare(c, carry):
            gather_chunk(c, carry)
            return norm_tiles(c, carry)

        lax.fori_loop(0, protos // 256, spread_center, 0)
        for load in loads:
            load.wait()
        lax.fori_loop(0, chunks, prepare, 0)

    pl.run_scoped(
        prologue,
        pltpu.VMEM((images, patches, width), BF16),
        pltpu.VMEM((images, patches, width), BF16),
        pltpu.VMEM((width, protos), BF16),
    )

    def copy(src, dst, send, recv, device):
        return pltpu.make_async_remote_copy(
            src_ref=src, dst_ref=dst, send_sem=send, recv_sem=recv, device_id=device,
            device_id_type=MESH,
        )

    def stat_x_copy(c, d):
        return copy(stat_x.at[c, 0], stat_x.at[c, d], sx_send, sx_recv.at[c], along_x(d))

    def stat_z_copy(c, d):
        return copy(stat_z.at[c, 0], stat_z.at[c, d], sz_send, sz_recv.at[c], along_z(d))

    def grad_x_copy(c, d):
        return copy(
            grad_x.at[c, lax.rem(x + d, nx)], got_x.at[c, d], gx_send, gx_recv.at[c], along_x(d)
        )

    def grad_z_copy(c, d):
        return copy(
            grad_z.at[c, lax.rem(z + d, nz)], got_z.at[c, d], gz_send, gz_recv.at[c], along_z(d)
        )

    def dp_copy(batch, d):
        n, at = batch
        return copy(
            own_dp.at[lax.rem(me + d, ndp), at], got_dp.at[me, at], dp_send, dp_recv.at[n],
            along_dp(d),
        )

    def all_z_copy(batch, d):
        n, at = batch
        block_ref = gathered.at[at, x, z]
        return copy(block_ref, block_ref, az_send, az_recv.at[n], along_z(d))

    def all_x_copy(batch, d):
        n, at = batch
        block_ref = gathered.at[at, x]
        return copy(block_ref, block_ref, ax_send, ax_recv.at[n], along_x(d))

    def loss_copy(d):
        return copy(losses.at[me], losses.at[me], lo_send, lo_recv, along_dp(d))

    def await_bytes(ref, sem):
        pltpu.make_async_copy(ref, ref, sem).wait()

    def statistics(s_exp, t_exp, c):
        slot = lax.rem(c, DEPTH)
        student = s_unit[c].reshape(rows, width)
        teacher = t_unit[c].reshape(rows, width)
        sums = [jnp.zeros((8, rows), F32)] * 3
        for n in range(0, protos, block):
            at = pl.ds(n, block)
            s = lax.dot_general(scols_t[at, :], student, NT, preferred_element_type=F32)
            t = lax.dot_general(tcols_t[at, :], teacher, NT, preferred_element_type=F32)
            shift = jnp.concatenate([center_b[at, :]] * (rows // 128), axis=1)
            es = jnp.exp2(s * (LOG2E / STUDENT_TEMP))
            et = jnp.exp2(t * (LOG2E / TEACHER_TEMP) - shift)
            s_exp[slot, at, :] = es
            t_exp[slot, at, :] = et
            sums = [
                total + jnp.sum(part.reshape(block // 8, 8, rows), axis=0)
                for total, part in zip(sums, (es, et, et * s))
            ]
        lines = [jnp.sum(total, axis=0, keepdims=True) for total in sums]
        stat_x[c, 0] = jnp.concatenate(lines + [jnp.zeros((1, rows), F32)], axis=0)
        for d in range(1, nx):
            stat_x_copy(c, d).start()

    def statistics_over_z(c):
        await_bytes(stat_x.at[c, 1:nx], sx_recv.at[c])
        total = stat_x[c, 0]
        for d in range(1, nx):
            total = total + stat_x[c, d]
        stat_z[c, 0] = total
        for d in range(1, nz):
            stat_z_copy(c, d).start()

    def gradient(s_exp, t_exp, c):
        slot = lax.rem(c, DEPTH)
        await_bytes(stat_z.at[c, 1:nz], sz_recv.at[c])
        total = stat_z[c, 0]
        for d in range(1, nz):
            total = total + stat_z[c, d]
        s_sum, t_sum, cross = total[0:1, :], total[1:2, :], total[2:3, :]
        loss = jnp.log(s_sum) - cross * (1.0 / STUDENT_TEMP) / t_sum
        losses[me, pl.ds(c, 1), :] = loss
        s_scale = (1.0 / STUDENT_TEMP) / s_sum
        t_scale = (1.0 / STUDENT_TEMP) / t_sum
        dz = jnp.zeros((width, rows), F32)
        for n in range(0, protos, block):
            at = pl.ds(n, block)
            dlogit = (s_exp[slot, at, :] * s_scale - t_exp[slot, at, :] * t_scale).astype(BF16)
            dz = dz + jnp.dot(scols[:, at], dlogit, preferred_element_type=F32)
        grad_x[c] = jnp.transpose(dz).reshape(nx, half, width)
        for d in range(1, nx):
            grad_x_copy(c, d).start()

    def gradient_over_z(c):
        for h in range(HALVES):
            u = c * HALVES + h
            await_bytes(got_x.at[u, 1:nx], gx_recv.at[u])
            total = grad_x[u, x]
            for d in range(1, nx):
                total = total + got_x[u, d]
            grad_z[c, :, h] = total.reshape(nz, unit_piece, width)
        for d in range(1, nz):
            grad_z_copy(c, d).start()

    def finish(c):
        await_bytes(got_z.at[c, 1:nz], gz_recv.at[c])
        dz = grad_z[c, z]
        for d in range(1, nz):
            dz = dz + got_z[c, d]
        dz = dz.reshape(piece, width)
        image = c * nx + x
        xs = s_in[image, pl.ds(pl.multiple_of(z * piece, piece), piece), :].astype(F32)
        norm = jnp.sqrt(jnp.sum(xs * xs, axis=1, keepdims=True) + EPSILON)
        inner = jnp.sum(xs * dz, axis=1, keepdims=True)
        dx = (dz / norm - xs * inner / (norm * norm * norm)).astype(BF16)
        before = iota(counts_ref.shape, 1) < me * images + image
        start = jnp.sum(jnp.where(before, counts_ref[...].astype(F32), 0.0), axis=1, keepdims=True)
        first = jnp.broadcast_to(start.astype(jnp.int32), (ndp * slot_rows, piece))
        pos = iota((ndp * slot_rows, piece), 0)
        k = iota((ndp * slot_rows, piece), 1)
        pick = (((first + k) % ndp) == pos // slot_rows) & (k // ndp == pos % slot_rows)
        sent = jnp.dot(pick.astype(F32).astype(BF16), dx, preferred_element_type=F32)
        own_dp[:, c] = sent.reshape(ndp, slot_rows, width)
        got_dp[me, c] = own_dp[me, c]

    def spread_dp(batch):
        for d in range(1, ndp):
            dp_copy(batch, d).start()

    def spread_z(batch):
        n, at = batch
        await_bytes(got_dp.at[0 : ndp - 1, at], dp_recv.at[n])
        pos = iota((piece, ndp * slot_rows), 0)
        k = iota((piece, ndp * slot_rows), 1)
        pick = (k // slot_rows == pos // per_res) & (k % slot_rows == pos % per_res)
        pick = pick.astype(F32).astype(BF16)
        for c in range(at.start, at.stop):
            held_rows = got_dp[:, c].reshape(ndp * slot_rows, width).astype(BF16)
            put = jnp.dot(pick, held_rows, preferred_element_type=F32)
            gathered[c, x, z] = put.astype(BF16)
        for d in range(1, nz):
            all_z_copy(batch, d).start()

    def spread_x(batch):
        n, at = batch
        await_bytes(gathered.at[at, x, 0 : nz - 1], az_recv.at[n])
        for d in range(1, nx):
            all_x_copy(batch, d).start()

    def index_rows():
        counts = counts_ref[...].astype(F32)
        upto = iota((total_images, total_images), 0) <= iota((total_images, total_images), 1)
        ends = jnp.dot(
            jnp.broadcast_to(counts, (8, total_images)).astype(BF16),
            upto.astype(F32).astype(BF16), preferred_element_type=F32,
        )[0:1, :]
        starts = ends - counts

        for n in range(mask_dev // tile):
            g = (n * tile + iota((tile, 1), 0)) * ndp + me
            wide = g.astype(F32)
            image = jnp.sum((wide >= ends).astype(F32), axis=1, keepdims=True).astype(jnp.int32)
            start = jnp.max(jnp.where(wide >= starts, starts, 0.0), axis=1, keepdims=True)
            j = g - start.astype(jnp.int32)
            owner, image = image // images, image % images
            at = (image * nz + j // piece) * piece + owner * per_res + (j % piece) // ndp
            lines = slice(n * tile, (n + 1) * tile)
            row_at[lines, :] = jnp.broadcast_to(at, (tile, 128))
            line = owner * units + (image // nx) * HALVES + (j // unit_piece) % HALVES
            lane = (image % nx) * half + (j // piece) * unit_piece + j % unit_piece
            row_key[lines, :] = jnp.broadcast_to(line * rows + lane, (tile, 128))

    def place(batch):
        n, chunk_at = batch
        await_bytes(gathered.at[chunk_at, 0 : nx - 1], ax_recv.at[n])
        first, count = chunk_at.start * held, (chunk_at.stop - chunk_at.start) * held
        values = gathered[chunk_at].reshape(count, width)
        for i in range(mask_dev // tile):
            lines = slice(i * tile, (i + 1) * tile)
            at = jnp.concatenate([row_at[lines, :] - first] * (count // 128), axis=1)
            pick = (iota((tile, count), 1) == at).astype(F32).astype(BF16)
            put = jnp.dot(pick, values, preferred_element_type=F32)
            if chunk_at.start > 0:
                put = put + grad[lines, :].astype(F32)
            grad[lines, :] = put.astype(BF16)

    def send_losses():
        for d in range(1, ndp):
            loss_copy(d).start()

    def place_losses():
        await_bytes(losses.at[0 : ndp - 1], lo_recv)
        wide = losses[...].reshape(ndp * units, rows)
        high = wide.astype(BF16)
        rest = wide - high.astype(F32)
        middle = rest.astype(BF16)
        low = (rest - middle.astype(F32)).astype(BF16)

        for n in range(mask_dev // tile):
            key = row_key[n * tile : (n + 1) * tile, :]
            line, lane = key // rows, key % rows
            pick = (iota((tile, 128), 1) == line).astype(F32).astype(BF16)[:, : ndp * units]
            lines = sum(
                jnp.dot(pick, part, preferred_element_type=F32) for part in (low, middle, high)
            )
            lane = jnp.concatenate([lane] * (rows // 128), axis=1)
            lines = jnp.where(iota((tile, rows), 1) == lane, lines, 0.0)
            row_loss[:, n * tile : (n + 1) * tile] = jnp.sum(
                jnp.transpose(lines), axis=0, keepdims=True
            )

    pl.semaphore_wait(barrier, len(partners))

    def pipeline(s_exp, t_exp):
        def step(t, carry):
            def at_lag(lag, work, every=1):
                u = t - lag

                @pl.when((u >= 0) & (u < units) & (lax.rem(u, every) == every - 1))
                def _():
                    work(u // every)

            at_lag(0, functools.partial(statistics, s_exp, t_exp))
            at_lag(1, statistics_over_z)
            at_lag(DEPTH - 1, functools.partial(gradient, s_exp, t_exp))
            at_lag(DEPTH + 1, gradient_over_z, HALVES)
            at_lag(DEPTH + 3, finish, HALVES)
            return carry

        lax.fori_loop(0, units + DEPTH - 1, step, 0)

    pl.run_scoped(
        pipeline,
        pltpu.VMEM((DEPTH, protos, rows), F32),
        pltpu.VMEM((DEPTH, protos, rows), F32),
    )
    last = chunks - 1
    send_losses()
    early = [(0, slice(0, last - 1))] if last > 1 else []
    before = (1, slice(last - 1, last))
    final = (2, slice(last, chunks))
    for batch in early:
        spread_dp(batch)
    index_rows()
    gradient_over_z(last)
    for batch in early:
        spread_z(batch)
    finish(last - 1)
    spread_dp(before)
    place_losses()
    for batch in early:
        spread_x(batch)
    finish(last)
    spread_dp(final)
    spread_z(before)
    spread_z(final)
    spread_x(before)
    for batch in early:
        place(batch)
    spread_x(final)
    place(before)
    place(final)
    await_bytes(stat_x.at[:, 1:nx], sx_send)
    await_bytes(stat_z.at[:, 1:nz], sz_send)
    await_bytes(got_x.at[:, 1:nx], gx_send)
    await_bytes(got_z.at[:, 1:nz], gz_send)
    await_bytes(got_dp.at[0 : ndp - 1], dp_send)
    await_bytes(gathered.at[:, x, 0 : nz - 1], az_send)
    await_bytes(gathered.at[:, 0 : nx - 1], ax_send)
    await_bytes(losses.at[0 : ndp - 1], lo_send)


def local(ndp, nz, nx, student_rows, teacher_rows, student_proto, teacher_proto, center, counts, order):
    images, patches, width = student_rows.shape
    slots = patches // 2
    protos = student_proto.shape[1]
    chunks = images // nx
    units = chunks * HALVES
    half = slots // HALVES
    rows = nx * half
    piece = slots // nz
    slot_rows = max(8, piece // ndp)
    mask_dev = counts.shape[0] * 96 // ndp
    tile = 256 if mask_dev % 256 == 0 else 128
    dims = (ndp, nz, nx, images, slots, min(512, protos), tile)
    any_spec = pl.BlockSpec(memory_space=pl.ANY)
    vmem = pl.BlockSpec(memory_space=pltpu.VMEM)
    dma = pltpu.SemaphoreType.DMA
    row_loss, grad = pl.pallas_call(
        functools.partial(head_kernel, dims),
        out_shape=(
            jax.ShapeDtypeStruct((1, mask_dev), F32),
            jax.ShapeDtypeStruct((mask_dev, width), BF16),
        ),
        in_specs=[any_spec] * 4 + [vmem] * 3,
        out_specs=(vmem, vmem),
        scratch_shapes=[
            pltpu.VMEM((width, protos), BF16),
            pltpu.VMEM((protos, width), BF16),
            pltpu.VMEM((protos, width), BF16),
            pltpu.VMEM((protos, 128), F32),
            pltpu.VMEM((images, slots, width), BF16),
            pltpu.VMEM((units, nx, half, width), BF16),
            pltpu.VMEM((units, nx, half, width), BF16),
            pltpu.VMEM((units, nx, 4, rows), F32),
            pltpu.VMEM((units, nz, 4, rows), F32),
            pltpu.VMEM((units, nx, half, width), F32),
            pltpu.VMEM((units, nx, half, width), F32),
            pltpu.VMEM((chunks, nz, HALVES, half // nz, width), F32),
            pltpu.VMEM((chunks, nz, HALVES, half // nz, width), F32),
            pltpu.VMEM((ndp, chunks, slot_rows, width), F32),
            pltpu.VMEM((ndp, chunks, slot_rows, width), F32),
            pltpu.VMEM((chunks, nx, nz, piece, width), BF16),
            pltpu.VMEM((ndp, units, rows), F32),
            pltpu.VMEM((mask_dev, 128), jnp.int32),
            pltpu.VMEM((mask_dev, 128), jnp.int32),
            dma((4,)),
            dma, dma((units,)),
            dma, dma((units,)),
            dma, dma((units,)),
            dma, dma((chunks,)),
            dma, dma((3,)),
            dma, dma((3,)),
            dma, dma((3,)),
            dma, dma,
        ],
        compiler_params=pltpu.CompilerParams(
            collective_id=0, has_side_effects=True, vmem_limit_bytes=63 * 2**20
        ),
        name="proto_head",
    )(student_rows, teacher_rows, student_proto, teacher_proto, center[None, :], counts[None, :], order)
    return row_loss, grad[None]


def solution(mesh):
    ndp, proto = mesh.shape["dp"], mesh.shape["proto"]
    nx = X_SIZE
    placed = (
        P("dp", None, None),
        P("dp", None, None),
        P(None, "proto"),
        P(None, "proto"),
        P("proto"),
        P(),
        P("dp", None),
    )
    return jax.shard_map(
        functools.partial(local, ndp, proto // nx, nx),
        mesh=mesh,
        in_specs=placed,
        out_specs=(P("dp", None), P("dp", None, None)),
        check_vma=False,
    )
```

```python
import functools
import math

import jax
import jax.numpy as jnp
from jax import lax
from jax.experimental import pallas as pl
from jax.experimental.pallas import tpu as pltpu
from jax.sharding import PartitionSpec as P

STUDENT_TEMP = 0.1
TEACHER_TEMP = 0.07
EPSILON = 1e-06
LOG2E = math.log2(math.e)
X_SIZE = 4
HALVES = 2
DEPTH = 4
F32 = jnp.float32
BF16 = jnp.bfloat16
MESH = pl.DeviceIdType.MESH
NT = (((1,), (1,)), ((), ()))
TN = (((0,), (0,)), ((), ()))


def iota(shape, dim):
    return lax.broadcasted_iota(jnp.int32, shape, dim)


def head_kernel(dims, *refs):
    ndp, nz, nx, images, slots, block, tile = dims
    (student_hbm, teacher_hbm, sproto_hbm, tproto_hbm, center_ref, counts_ref, order_ref,
     row_loss, grad,
     scols, scols_t, tcols_t, center_b, s_in, s_unit, t_unit, stat_x, stat_z, grad_x, got_x,
     grad_z, got_z, own_dp, got_dp, gathered, losses, row_at, row_key,
     load_sem, sx_send, sx_recv, sz_send, sz_recv, gx_send, gx_recv, gz_send, gz_recv,
     dp_send, dp_recv, az_send, az_recv, ax_send, ax_recv, lo_send, lo_recv) = refs
    chunks = images // nx
    units = chunks * HALVES
    half = slots // HALVES
    rows = nx * half
    piece = slots // nz
    unit_piece = half // nz
    per_res = piece // ndp
    slot_rows = own_dp.shape[2]
    protos = scols.shape[1]
    width = scols.shape[0]
    patches = order_ref.shape[1]
    total_images = counts_ref.shape[1]
    mask_dev = grad.shape[0]
    held = nx * nz * piece
    me = lax.axis_index("dp")
    q = lax.axis_index("proto")
    z = q // nx
    x = q % nx

    def along_x(d):
        return (me, z * nx + lax.rem(x + d, nx))

    def along_z(d):
        return (me, lax.rem(z + d, nz) * nx + x)

    def along_dp(d):
        return (lax.rem(me + d, ndp), q)

    barrier = pltpu.get_barrier_semaphore()
    partners = (
        [along_x(d) for d in range(1, nx)]
        + [along_z(d) for d in range(1, nz)]
        + [along_dp(d) for d in range(1, ndp)]
    )
    for partner in partners:
        pl.semaphore_signal(barrier, inc=1, device_id=partner, device_id_type=MESH)

    def prologue(srows, trows, tcols):
        loads = [
            pltpu.make_async_copy(src, dst, load_sem.at[i])
            for i, (src, dst) in enumerate(
                ((student_hbm, srows), (teacher_hbm, trows), (sproto_hbm, scols), (tproto_hbm, tcols))
            )
        ]
        for load in loads:
            load.start()

        def spread_center(n, carry):
            for i in range(spread):
                at = pl.ds(pl.multiple_of((n * spread + i) * 128, 128), 128)
                row = center_ref[:, at] * (LOG2E / TEACHER_TEMP)
                center_b[at, :] = jnp.transpose(jnp.broadcast_to(row, (128, 128)))
            return carry

        def gather_chunk(c, carry):
            for i in range(nx):
                image = c * nx + i
                order = order_ref[pl.ds(image, 1), :][:, :slots]
                pick = (iota((patches, slots), 0) == order).astype(F32).astype(BF16)
                for source, units_ref in ((srows, s_unit), (trows, t_unit)):
                    wide = lax.dot_general(pick, source[image], TN, preferred_element_type=F32)
                    if source is srows:
                        s_in[image] = wide.astype(BF16)
                    norm = jnp.sqrt(jnp.sum(wide * wide, axis=1, keepdims=True) + EPSILON)
                    unit = (wide / norm).reshape(nz, HALVES, unit_piece, width)
                    for h in range(HALVES):
                        units_ref[c * HALVES + h, i] = unit[:, h].reshape(half, width).astype(BF16)
            return carry

        def norm_tiles(n, carry):
            for i in range(group):
                at = pl.ds(pl.multiple_of((n * group + i) * 256, 256), 256)
                for cols, turned in ((scols, scols_t), (tcols, tcols_t)):
                    wide = cols[:, at].astype(F32)
                    scale = 1.0 / jnp.sqrt(jnp.sum(wide * wide, axis=0, keepdims=True) + EPSILON)
                    unit = (wide * scale).astype(BF16)
                    if cols is scols:
                        cols[:, at] = unit
                    turned[at, :] = jnp.transpose(unit)
            return carry

        spread = min(8, protos // 128)
        group = min(4, protos // 256)
        lax.fori_loop(0, protos // (128 * spread), spread_center, 0)
        loads[0].wait()
        loads[1].wait()
        lax.fori_loop(0, chunks, gather_chunk, 0)
        loads[2].wait()
        loads[3].wait()
        lax.fori_loop(0, protos // (256 * group), norm_tiles, 0)

    pl.run_scoped(
        prologue,
        pltpu.VMEM((images, patches, width), BF16),
        pltpu.VMEM((images, patches, width), BF16),
        pltpu.VMEM((width, protos), BF16),
    )

    def copy(src, dst, send, recv, device):
        return pltpu.make_async_remote_copy(
            src_ref=src, dst_ref=dst, send_sem=send, recv_sem=recv, device_id=device,
            device_id_type=MESH,
        )

    def stat_x_copy(c, d):
        return copy(stat_x.at[c, 0], stat_x.at[c, d], sx_send, sx_recv.at[c], along_x(d))

    def stat_z_copy(c, d):
        return copy(stat_z.at[c, 0], stat_z.at[c, d], sz_send, sz_recv.at[c], along_z(d))

    def grad_x_copy(c, d):
        return copy(
            grad_x.at[c, lax.rem(x + d, nx)], got_x.at[c, d], gx_send, gx_recv.at[c], along_x(d)
        )

    def grad_z_copy(c, d):
        return copy(
            grad_z.at[c, lax.rem(z + d, nz)], got_z.at[c, d], gz_send, gz_recv.at[c], along_z(d)
        )

    def dp_copy(batch, d):
        n, at = batch
        return copy(
            own_dp.at[lax.rem(me + d, ndp), at], got_dp.at[me, at], dp_send, dp_recv.at[n],
            along_dp(d),
        )

    def all_z_copy(batch, d):
        n, at = batch
        block_ref = gathered.at[at, x, z]
        return copy(block_ref, block_ref, az_send, az_recv.at[n], along_z(d))

    def all_x_copy(batch, d):
        n, at = batch
        block_ref = gathered.at[at, x]
        return copy(block_ref, block_ref, ax_send, ax_recv.at[n], along_x(d))

    def loss_copy(d):
        return copy(losses.at[me], losses.at[me], lo_send, lo_recv, along_dp(d))

    def await_bytes(ref, sem):
        pltpu.make_async_copy(ref, ref, sem).wait()

    def statistics(s_exp, t_exp, c):
        slot = lax.rem(c, DEPTH)
        student = s_unit[c].reshape(rows, width)
        teacher = t_unit[c].reshape(rows, width)
        sums = [jnp.zeros((8, rows), F32)] * 3
        for n in range(0, protos, block):
            at = pl.ds(n, block)
            s = lax.dot_general(scols_t[at, :], student, NT, preferred_element_type=F32)
            t = lax.dot_general(tcols_t[at, :], teacher, NT, preferred_element_type=F32)
            shift = jnp.concatenate([center_b[at, :]] * (rows // 128), axis=1)
            es = jnp.exp2(s * (LOG2E / STUDENT_TEMP))
            et = jnp.exp2(t * (LOG2E / TEACHER_TEMP) - shift)
            s_exp[slot, at, :] = es
            t_exp[slot, at, :] = et
            sums = [
                total + jnp.sum(part.reshape(block // 8, 8, rows), axis=0)
                for total, part in zip(sums, (es, et, et * s))
            ]
        lines = [jnp.sum(total, axis=0, keepdims=True) for total in sums]
        stat_x[c, 0] = jnp.concatenate(lines + [jnp.zeros((1, rows), F32)], axis=0)
        for d in range(1, nx):
            stat_x_copy(c, d).start()

    def statistics_over_z(c):
        await_bytes(stat_x.at[c, 1:nx], sx_recv.at[c])
        total = stat_x[c, 0]
        for d in range(1, nx):
            total = total + stat_x[c, d]
        stat_z[c, 0] = total
        for d in range(1, nz):
            stat_z_copy(c, d).start()

    def gradient(s_exp, t_exp, c):
        slot = lax.rem(c, DEPTH)
        await_bytes(stat_z.at[c, 1:nz], sz_recv.at[c])
        total = stat_z[c, 0]
        for d in range(1, nz):
            total = total + stat_z[c, d]
        s_sum, t_sum, cross = total[0:1, :], total[1:2, :], total[2:3, :]
        loss = jnp.log(s_sum) - cross * (1.0 / STUDENT_TEMP) / t_sum
        losses[me, pl.ds(c, 1), :] = loss
        s_scale = (1.0 / STUDENT_TEMP) / s_sum
        t_scale = (1.0 / STUDENT_TEMP) / t_sum
        dz = jnp.zeros((width, rows), F32)
        for n in range(0, protos, block):
            at = pl.ds(n, block)
            dlogit = (s_exp[slot, at, :] * s_scale - t_exp[slot, at, :] * t_scale).astype(BF16)
            dz = dz + jnp.dot(scols[:, at], dlogit, preferred_element_type=F32)
        grad_x[c] = jnp.transpose(dz).reshape(nx, half, width)
        for d in range(1, nx):
            grad_x_copy(c, d).start()

    def gradient_over_z(c):
        for h in range(HALVES):
            u = c * HALVES + h
            await_bytes(got_x.at[u, 1:nx], gx_recv.at[u])
            total = grad_x[u, x]
            for d in range(1, nx):
                total = total + got_x[u, d]
            grad_z[c, :, h] = total.reshape(nz, unit_piece, width)
        for d in range(1, nz):
            grad_z_copy(c, d).start()

    def finish(c):
        await_bytes(got_z.at[c, 1:nz], gz_recv.at[c])
        dz = grad_z[c, z]
        for d in range(1, nz):
            dz = dz + got_z[c, d]
        dz = dz.reshape(piece, width)
        image = c * nx + x
        xs = s_in[image, pl.ds(pl.multiple_of(z * piece, piece), piece), :].astype(F32)
        norm = jnp.sqrt(jnp.sum(xs * xs, axis=1, keepdims=True) + EPSILON)
        inner = jnp.sum(xs * dz, axis=1, keepdims=True)
        dx = (dz / norm - xs * inner / (norm * norm * norm)).astype(BF16)
        before = iota(counts_ref.shape, 1) < me * images + image
        start = jnp.sum(jnp.where(before, counts_ref[...].astype(F32), 0.0), axis=1, keepdims=True)
        first = jnp.broadcast_to(start.astype(jnp.int32), (ndp * slot_rows, piece))
        pos = iota((ndp * slot_rows, piece), 0)
        k = iota((ndp * slot_rows, piece), 1)
        pick = (((first + k) % ndp) == pos // slot_rows) & (k // ndp == pos % slot_rows)
        sent = jnp.dot(pick.astype(F32).astype(BF16), dx, preferred_element_type=F32)
        own_dp[:, c] = sent.reshape(ndp, slot_rows, width)
        got_dp[me, c] = own_dp[me, c]

    def spread_dp(batch):
        for d in range(1, ndp):
            dp_copy(batch, d).start()

    def spread_z(batch):
        n, at = batch
        await_bytes(got_dp.at[0 : ndp - 1, at], dp_recv.at[n])
        pos = iota((piece, ndp * slot_rows), 0)
        k = iota((piece, ndp * slot_rows), 1)
        pick = (k // slot_rows == pos // per_res) & (k % slot_rows == pos % per_res)
        pick = pick.astype(F32).astype(BF16)
        for c in range(at.start, at.stop):
            held_rows = got_dp[:, c].reshape(ndp * slot_rows, width).astype(BF16)
            put = jnp.dot(pick, held_rows, preferred_element_type=F32)
            gathered[c, x, z] = put.astype(BF16)
        for d in range(1, nz):
            all_z_copy(batch, d).start()

    def spread_x(batch):
        n, at = batch
        await_bytes(gathered.at[at, x, 0 : nz - 1], az_recv.at[n])
        for d in range(1, nx):
            all_x_copy(batch, d).start()

    def index_rows():
        counts = counts_ref[...].astype(F32)
        upto = iota((total_images, total_images), 0) <= iota((total_images, total_images), 1)
        ends = jnp.dot(
            jnp.broadcast_to(counts, (8, total_images)).astype(BF16),
            upto.astype(F32).astype(BF16), preferred_element_type=F32,
        )[0:1, :]
        starts = ends - counts

        for n in range(mask_dev // tile):
            g = (n * tile + iota((tile, 1), 0)) * ndp + me
            wide = g.astype(F32)
            image = jnp.sum((wide >= ends).astype(F32), axis=1, keepdims=True).astype(jnp.int32)
            start = jnp.max(jnp.where(wide >= starts, starts, 0.0), axis=1, keepdims=True)
            j = g - start.astype(jnp.int32)
            owner, image = image // images, image % images
            at = (image * nz + j // piece) * piece + owner * per_res + (j % piece) // ndp
            lines = slice(n * tile, (n + 1) * tile)
            row_at[lines, :] = jnp.broadcast_to(at, (tile, 128))
            line = owner * units + (image // nx) * HALVES + (j // unit_piece) % HALVES
            lane = (image % nx) * half + (j // piece) * unit_piece + j % unit_piece
            row_key[lines, :] = jnp.broadcast_to(line * rows + lane, (tile, 128))

    def place(batch):
        n, chunk_at = batch
        await_bytes(gathered.at[chunk_at, 0 : nx - 1], ax_recv.at[n])
        first, count = chunk_at.start * held, (chunk_at.stop - chunk_at.start) * held
        values = gathered[chunk_at].reshape(count, width)
        for i in range(mask_dev // tile):
            lines = slice(i * tile, (i + 1) * tile)
            at = jnp.concatenate([row_at[lines, :] - first] * (count // 128), axis=1)
            pick = (iota((tile, count), 1) == at).astype(F32).astype(BF16)
            put = jnp.dot(pick, values, preferred_element_type=F32)
            if chunk_at.start > 0:
                put = put + grad[lines, :].astype(F32)
            grad[lines, :] = put.astype(BF16)

    def send_losses():
        for d in range(1, ndp):
            loss_copy(d).start()

    def place_losses():
        await_bytes(losses.at[0 : ndp - 1], lo_recv)
        wide = losses[...].reshape(ndp * units, rows)
        high = wide.astype(BF16)
        rest = wide - high.astype(F32)
        middle = rest.astype(BF16)
        low = (rest - middle.astype(F32)).astype(BF16)

        for n in range(mask_dev // tile):
            key = row_key[n * tile : (n + 1) * tile, :]
            line, lane = key // rows, key % rows
            pick = (iota((tile, 128), 1) == line).astype(F32).astype(BF16)[:, : ndp * units]
            lines = sum(
                jnp.dot(pick, part, preferred_element_type=F32) for part in (low, middle, high)
            )
            lane = jnp.concatenate([lane] * (rows // 128), axis=1)
            lines = jnp.where(iota((tile, rows), 1) == lane, lines, 0.0)
            row_loss[:, n * tile : (n + 1) * tile] = jnp.sum(
                jnp.transpose(lines), axis=0, keepdims=True
            )

    pl.semaphore_wait(barrier, len(partners))

    def pipeline(s_exp, t_exp):
        def step(t, carry):
            def at_lag(lag, work, every=1):
                u = t - lag

                @pl.when((u >= 0) & (u < units) & (lax.rem(u, every) == every - 1))
                def _():
                    work(u // every)

            at_lag(0, functools.partial(statistics, s_exp, t_exp))
            at_lag(1, statistics_over_z)
            at_lag(DEPTH - 1, functools.partial(gradient, s_exp, t_exp))
            at_lag(DEPTH + 1, gradient_over_z, HALVES)
            at_lag(DEPTH + 3, finish, HALVES)
            return carry

        lax.fori_loop(0, units + DEPTH - 1, step, 0)

    pl.run_scoped(
        pipeline,
        pltpu.VMEM((DEPTH, protos, rows), F32),
        pltpu.VMEM((DEPTH, protos, rows), F32),
    )
    last = chunks - 1
    send_losses()
    early = [(0, slice(0, last - 1))] if last > 1 else []
    before = (1, slice(last - 1, last))
    final = (2, slice(last, chunks))
    for batch in early:
        spread_dp(batch)
    index_rows()
    gradient_over_z(last)
    for batch in early:
        spread_z(batch)
    finish(last - 1)
    spread_dp(before)
    for batch in early:
        spread_x(batch)
    finish(last)
    spread_dp(final)
    spread_z(before)
    spread_z(final)
    spread_x(before)
    for batch in early:
        place(batch)
    place_losses()
    spread_x(final)
    place(before)
    place(final)
    await_bytes(stat_x.at[:, 1:nx], sx_send)
    await_bytes(stat_z.at[:, 1:nz], sz_send)
    await_bytes(got_x.at[:, 1:nx], gx_send)
    await_bytes(got_z.at[:, 1:nz], gz_send)
    await_bytes(got_dp.at[0 : ndp - 1], dp_send)
    await_bytes(gathered.at[:, x, 0 : nz - 1], az_send)
    await_bytes(gathered.at[:, 0 : nx - 1], ax_send)
    await_bytes(losses.at[0 : ndp - 1], lo_send)


def hand_over_kernel(loss, grad, row_loss, student_grad, sem):
    copies = [
        pltpu.make_async_copy(loss, row_loss, sem.at[0]),
        pltpu.make_async_copy(grad, student_grad.at[0], sem.at[1]),
    ]
    for each in copies:
        each.start()
    for each in copies:
        each.wait()


def local(ndp, nz, nx, student_rows, teacher_rows, student_proto, teacher_proto, center, counts, order):
    images, patches, width = student_rows.shape
    slots = patches // 2
    protos = student_proto.shape[1]
    chunks = images // nx
    units = chunks * HALVES
    half = slots // HALVES
    rows = nx * half
    piece = slots // nz
    slot_rows = max(8, piece // ndp)
    mask_dev = counts.shape[0] * 96 // ndp
    tile = 256 if mask_dev % 256 == 0 else 128
    dims = (ndp, nz, nx, images, slots, min(512, protos), tile)
    any_spec = pl.BlockSpec(memory_space=pl.ANY)
    vmem = pl.BlockSpec(memory_space=pltpu.VMEM)
    dma = pltpu.SemaphoreType.DMA
    row_loss, grad = pl.pallas_call(
        functools.partial(head_kernel, dims),
        out_shape=(
            jax.ShapeDtypeStruct((1, mask_dev), F32),
            jax.ShapeDtypeStruct((mask_dev, width), BF16),
        ),
        in_specs=[any_spec] * 4 + [vmem] * 3,
        out_specs=(vmem, vmem),
        scratch_shapes=[
            pltpu.VMEM((width, protos), BF16),
            pltpu.VMEM((protos, width), BF16),
            pltpu.VMEM((protos, width), BF16),
            pltpu.VMEM((protos, 128), F32),
            pltpu.VMEM((images, slots, width), BF16),
            pltpu.VMEM((units, nx, half, width), BF16),
            pltpu.VMEM((units, nx, half, width), BF16),
            pltpu.VMEM((units, nx, 4, rows), F32),
            pltpu.VMEM((units, nz, 4, rows), F32),
            pltpu.VMEM((units, nx, half, width), F32),
            pltpu.VMEM((units, nx, half, width), F32),
            pltpu.VMEM((chunks, nz, HALVES, half // nz, width), F32),
            pltpu.VMEM((chunks, nz, HALVES, half // nz, width), F32),
            pltpu.VMEM((ndp, chunks, slot_rows, width), F32),
            pltpu.VMEM((ndp, chunks, slot_rows, width), F32),
            pltpu.VMEM((chunks, nx, nz, piece, width), BF16),
            pltpu.VMEM((ndp, units, rows), F32),
            pltpu.VMEM((mask_dev, 128), jnp.int32),
            pltpu.VMEM((mask_dev, 128), jnp.int32),
            dma((4,)),
            dma, dma((units,)),
            dma, dma((units,)),
            dma, dma((units,)),
            dma, dma((chunks,)),
            dma, dma((3,)),
            dma, dma((3,)),
            dma, dma((3,)),
            dma, dma,
        ],
        compiler_params=pltpu.CompilerParams(
            collective_id=0, has_side_effects=True, vmem_limit_bytes=63 * 2**20
        ),
        name="proto_head",
    )(student_rows, teacher_rows, student_proto, teacher_proto, center[None, :], counts[None, :], order)
    return pl.pallas_call(
        hand_over_kernel,
        out_shape=(
            jax.ShapeDtypeStruct((1, mask_dev), F32),
            jax.ShapeDtypeStruct((1, mask_dev, width), BF16),
        ),
        in_specs=[any_spec] * 2,
        out_specs=(any_spec, any_spec),
        scratch_shapes=[dma((2,))],
        name="hand_over",
    )(row_loss, grad)


def solution(mesh):
    ndp, proto = mesh.shape["dp"], mesh.shape["proto"]
    nx = X_SIZE
    placed = (
        P("dp", None, None),
        P("dp", None, None),
        P(None, "proto"),
        P(None, "proto"),
        P("proto"),
        P(),
        P("dp", None),
    )
    return jax.shard_map(
        functools.partial(local, ndp, proto // nx, nx),
        mesh=mesh,
        in_specs=placed,
        out_specs=(P("dp", None), P("dp", None, None)),
        check_vma=False,
    )
```

```python
import functools
import math

import jax
import jax.numpy as jnp
from jax import lax
from jax.experimental import pallas as pl
from jax.experimental.pallas import tpu as pltpu
from jax.sharding import PartitionSpec as P

STUDENT_TEMP = 0.1
TEACHER_TEMP = 0.07
EPSILON = 1e-06
LOG2E = math.log2(math.e)
X_SIZE = 4
Z_NEAR = 4
HALVES = 2
DEPTH = 4
F32 = jnp.float32
BF16 = jnp.bfloat16
MESH = pl.DeviceIdType.MESH
NT = (((1,), (1,)), ((), ()))
TN = (((0,), (0,)), ((), ()))


def iota(shape, dim):
    return lax.broadcasted_iota(jnp.int32, shape, dim)


def head_kernel(dims, *refs):
    ndp, nz, nx, images, slots, block, tile = dims
    (student_hbm, teacher_hbm, sproto_hbm, tproto_hbm, center_ref, counts_ref, order_ref,
     row_loss, grad,
     scols, scols_t, tcols_t, center_b, s_in, s_unit, t_unit, stat_x, stat_z, stat_f, grad_x, got_x,
     grad_z, got_z, own_dp, got_dp, gathered, losses, row_at, row_key,
     load_sem, sx_send, sx_recv, sz_send, sz_recv, sf_send, sf_recv, gx_send, gx_recv, gz_send, gz_recv,
     dp_send, dp_recv, az_send, az_recv, ax_send, ax_recv, lo_send, lo_recv) = refs
    chunks = images // nx
    units = chunks * HALVES
    half = slots // HALVES
    rows = nx * half
    piece = slots // nz
    unit_piece = half // nz
    per_res = piece // ndp
    slot_rows = own_dp.shape[2]
    protos = scols.shape[1]
    width = scols.shape[0]
    patches = order_ref.shape[1]
    total_images = counts_ref.shape[1]
    mask_dev = grad.shape[0]
    held = nx * nz * piece
    me = lax.axis_index("dp")
    q = lax.axis_index("proto")
    z = q // nx
    x = q % nx

    def along_x(d):
        return (me, z * nx + lax.rem(x + d, nx))

    def along_z(d):
        return (me, lax.rem(z + d, nz) * nx + x)

    def along_near(d):
        return (me, (z // Z_NEAR * Z_NEAR + lax.rem(z % Z_NEAR + d, Z_NEAR)) * nx + x)

    def along_far(d):
        return along_z(d * Z_NEAR)

    def along_dp(d):
        return (lax.rem(me + d, ndp), q)

    barrier = pltpu.get_barrier_semaphore()
    partners = (
        [along_x(d) for d in range(1, nx)]
        + [along_z(d) for d in range(1, nz)]
        + [along_dp(d) for d in range(1, ndp)]
    )
    for partner in partners:
        pl.semaphore_signal(barrier, inc=1, device_id=partner, device_id_type=MESH)

    def prologue(srows, trows, tcols):
        loads = [
            pltpu.make_async_copy(src, dst, load_sem.at[i])
            for i, (src, dst) in enumerate(
                ((student_hbm, srows), (teacher_hbm, trows), (sproto_hbm, scols), (tproto_hbm, tcols))
            )
        ]
        for load in loads:
            load.start()

        def spread_center(n, carry):
            for i in range(spread):
                at = pl.ds(pl.multiple_of((n * spread + i) * 128, 128), 128)
                row = center_ref[:, at] * (LOG2E / TEACHER_TEMP)
                center_b[at, :] = jnp.transpose(jnp.broadcast_to(row, (128, 128)))
            return carry

        def gather_chunk(c, carry):
            for i in range(nx):
                image = c * nx + i
                order = order_ref[pl.ds(image, 1), :][:, :slots]
                pick = (iota((patches, slots), 0) == order).astype(F32).astype(BF16)
                for source, units_ref in ((srows, s_unit), (trows, t_unit)):
                    wide = lax.dot_general(pick, source[image], TN, preferred_element_type=F32)
                    if source is srows:
                        s_in[image] = wide.astype(BF16)
                    norm = jnp.sqrt(jnp.sum(wide * wide, axis=1, keepdims=True) + EPSILON)
                    unit = (wide / norm).reshape(nz, HALVES, unit_piece, width)
                    for h in range(HALVES):
                        units_ref[c * HALVES + h, i] = unit[:, h].reshape(half, width).astype(BF16)
            return carry

        def norm_tiles(n, carry):
            for i in range(group):
                at = pl.ds(pl.multiple_of((n * group + i) * 256, 256), 256)
                for cols, turned in ((scols, scols_t), (tcols, tcols_t)):
                    wide = cols[:, at].astype(F32)
                    scale = 1.0 / jnp.sqrt(jnp.sum(wide * wide, axis=0, keepdims=True) + EPSILON)
                    unit = (wide * scale).astype(BF16)
                    if cols is scols:
                        cols[:, at] = unit
                    turned[at, :] = jnp.transpose(unit)
            return carry

        spread = min(8, protos // 128)
        group = min(4, protos // 256)
        lax.fori_loop(0, protos // (128 * spread), spread_center, 0)
        loads[0].wait()
        loads[1].wait()
        lax.fori_loop(0, chunks, gather_chunk, 0)
        loads[2].wait()
        loads[3].wait()
        lax.fori_loop(0, protos // (256 * group), norm_tiles, 0)

    pl.run_scoped(
        prologue,
        pltpu.VMEM((images, patches, width), BF16),
        pltpu.VMEM((images, patches, width), BF16),
        pltpu.VMEM((width, protos), BF16),
    )

    def copy(src, dst, send, recv, device):
        return pltpu.make_async_remote_copy(
            src_ref=src, dst_ref=dst, send_sem=send, recv_sem=recv, device_id=device,
            device_id_type=MESH,
        )

    def stat_x_copy(c, d):
        return copy(stat_x.at[c, 0], stat_x.at[c, d], sx_send, sx_recv.at[c], along_x(d))

    def stat_z_copy(c, d):
        return copy(stat_z.at[c, 0], stat_z.at[c, d], sz_send, sz_recv.at[c], along_near(d))

    def stat_f_copy(c, d):
        return copy(stat_f.at[c, 0], stat_f.at[c, d], sf_send, sf_recv.at[c], along_far(d))

    def grad_x_copy(c, d):
        return copy(
            grad_x.at[c, lax.rem(x + d, nx)], got_x.at[c, d], gx_send, gx_recv.at[c], along_x(d)
        )

    def grad_z_copy(c, d):
        return copy(
            grad_z.at[c, lax.rem(z + d, nz)], got_z.at[c, d], gz_send, gz_recv.at[c], along_z(d)
        )

    def dp_copy(batch, d):
        n, at = batch
        return copy(
            own_dp.at[lax.rem(me + d, ndp), at], got_dp.at[me, at], dp_send, dp_recv.at[n],
            along_dp(d),
        )

    def all_z_copy(batch, d):
        n, at = batch
        block_ref = gathered.at[at, x, z]
        return copy(block_ref, block_ref, az_send, az_recv.at[n], along_z(d))

    def all_x_copy(batch, d):
        n, at = batch
        block_ref = gathered.at[at, x]
        return copy(block_ref, block_ref, ax_send, ax_recv.at[n], along_x(d))

    def loss_copy(d):
        return copy(losses.at[me], losses.at[me], lo_send, lo_recv, along_dp(d))

    def await_bytes(ref, sem):
        pltpu.make_async_copy(ref, ref, sem).wait()

    def statistics(s_exp, t_exp, c):
        slot = lax.rem(c, DEPTH)
        student = s_unit[c].reshape(rows, width)
        teacher = t_unit[c].reshape(rows, width)
        sums = [jnp.zeros((8, rows), F32)] * 3
        for n in range(0, protos, block):
            at = pl.ds(n, block)
            s = lax.dot_general(scols_t[at, :], student, NT, preferred_element_type=F32)
            t = lax.dot_general(tcols_t[at, :], teacher, NT, preferred_element_type=F32)
            shift = jnp.concatenate([center_b[at, :]] * (rows // 128), axis=1)
            es = jnp.exp2(s * (LOG2E / STUDENT_TEMP))
            et = jnp.exp2(t * (LOG2E / TEACHER_TEMP) - shift)
            s_exp[slot, at, :] = es
            t_exp[slot, at, :] = et
            sums = [
                total + jnp.sum(part.reshape(block // 8, 8, rows), axis=0)
                for total, part in zip(sums, (es, et, et * s))
            ]
        lines = [jnp.sum(total, axis=0, keepdims=True) for total in sums]
        stat_x[c, 0] = jnp.concatenate(lines + [jnp.zeros((1, rows), F32)], axis=0)
        for d in range(1, nx):
            stat_x_copy(c, d).start()

    def statistics_over_z(c):
        await_bytes(stat_x.at[c, 1:nx], sx_recv.at[c])
        total = stat_x[c, 0]
        for d in range(1, nx):
            total = total + stat_x[c, d]
        stat_z[c, 0] = total
        for d in range(1, Z_NEAR):
            stat_z_copy(c, d).start()

    def statistics_over_far(c):
        await_bytes(stat_z.at[c, 1:Z_NEAR], sz_recv.at[c])
        total = stat_z[c, 0]
        for d in range(1, Z_NEAR):
            total = total + stat_z[c, d]
        stat_f[c, 0] = total
        for d in range(1, nz // Z_NEAR):
            stat_f_copy(c, d).start()

    def gradient(s_exp, t_exp, c):
        slot = lax.rem(c, DEPTH)
        await_bytes(stat_f.at[c, 1 : nz // Z_NEAR], sf_recv.at[c])
        total = stat_f[c, 0]
        for d in range(1, nz // Z_NEAR):
            total = total + stat_f[c, d]
        s_sum, t_sum, cross = total[0:1, :], total[1:2, :], total[2:3, :]
        loss = jnp.log(s_sum) - cross * (1.0 / STUDENT_TEMP) / t_sum
        losses[me, pl.ds(c, 1), :] = loss
        s_scale = (1.0 / STUDENT_TEMP) / s_sum
        t_scale = (1.0 / STUDENT_TEMP) / t_sum
        dz = jnp.zeros((width, rows), F32)
        for n in range(0, protos, block):
            at = pl.ds(n, block)
            dlogit = (s_exp[slot, at, :] * s_scale - t_exp[slot, at, :] * t_scale).astype(BF16)
            dz = dz + jnp.dot(scols[:, at], dlogit, preferred_element_type=F32)
        grad_x[c] = jnp.transpose(dz).reshape(nx, half, width)
        for d in range(1, nx):
            grad_x_copy(c, d).start()

    def gradient_over_z(c):
        for h in range(HALVES):
            u = c * HALVES + h
            await_bytes(got_x.at[u, 1:nx], gx_recv.at[u])
            total = grad_x[u, x]
            for d in range(1, nx):
                total = total + got_x[u, d]
            grad_z[c, :, h] = total.reshape(nz, unit_piece, width)
        for d in range(1, nz):
            grad_z_copy(c, d).start()

    def finish(c):
        await_bytes(got_z.at[c, 1:nz], gz_recv.at[c])
        dz = grad_z[c, z]
        for d in range(1, nz):
            dz = dz + got_z[c, d]
        dz = dz.reshape(piece, width)
        image = c * nx + x
        xs = s_in[image, pl.ds(pl.multiple_of(z * piece, piece), piece), :].astype(F32)
        norm = jnp.sqrt(jnp.sum(xs * xs, axis=1, keepdims=True) + EPSILON)
        inner = jnp.sum(xs * dz, axis=1, keepdims=True)
        dx = (dz / norm - xs * inner / (norm * norm * norm)).astype(BF16)
        before = iota(counts_ref.shape, 1) < me * images + image
        start = jnp.sum(jnp.where(before, counts_ref[...].astype(F32), 0.0), axis=1, keepdims=True)
        first = jnp.broadcast_to(start.astype(jnp.int32), (ndp * slot_rows, piece))
        pos = iota((ndp * slot_rows, piece), 0)
        k = iota((ndp * slot_rows, piece), 1)
        pick = (((first + k) % ndp) == pos // slot_rows) & (k // ndp == pos % slot_rows)
        sent = jnp.dot(pick.astype(F32).astype(BF16), dx, preferred_element_type=F32)
        own_dp[:, c] = sent.reshape(ndp, slot_rows, width)
        got_dp[me, c] = own_dp[me, c]

    def spread_dp(batch):
        for d in range(1, ndp):
            dp_copy(batch, d).start()

    def spread_z(batch):
        n, at = batch
        await_bytes(got_dp.at[0 : ndp - 1, at], dp_recv.at[n])
        pos = iota((piece, ndp * slot_rows), 0)
        k = iota((piece, ndp * slot_rows), 1)
        pick = (k // slot_rows == pos // per_res) & (k % slot_rows == pos % per_res)
        pick = pick.astype(F32).astype(BF16)
        for c in range(at.start, at.stop):
            held_rows = got_dp[:, c].reshape(ndp * slot_rows, width).astype(BF16)
            put = jnp.dot(pick, held_rows, preferred_element_type=F32)
            gathered[c, x, z] = put.astype(BF16)
        for d in range(1, nz):
            all_z_copy(batch, d).start()

    def spread_x(batch):
        n, at = batch
        await_bytes(gathered.at[at, x, 0 : nz - 1], az_recv.at[n])
        for d in range(1, nx):
            all_x_copy(batch, d).start()

    def index_rows():
        counts = counts_ref[...].astype(F32)
        upto = iota((total_images, total_images), 0) <= iota((total_images, total_images), 1)
        ends = jnp.dot(
            jnp.broadcast_to(counts, (8, total_images)).astype(BF16),
            upto.astype(F32).astype(BF16), preferred_element_type=F32,
        )[0:1, :]
        starts = ends - counts

        for n in range(mask_dev // tile):
            g = (n * tile + iota((tile, 1), 0)) * ndp + me
            wide = g.astype(F32)
            image = jnp.sum((wide >= ends).astype(F32), axis=1, keepdims=True).astype(jnp.int32)
            start = jnp.max(jnp.where(wide >= starts, starts, 0.0), axis=1, keepdims=True)
            j = g - start.astype(jnp.int32)
            owner, image = image // images, image % images
            at = (image * nz + j // piece) * piece + owner * per_res + (j % piece) // ndp
            lines = slice(n * tile, (n + 1) * tile)
            row_at[lines, :] = jnp.broadcast_to(at, (tile, 128))
            line = owner * units + (image // nx) * HALVES + (j // unit_piece) % HALVES
            lane = (image % nx) * half + (j // piece) * unit_piece + j % unit_piece
            row_key[lines, :] = jnp.broadcast_to(line * rows + lane, (tile, 128))

    def place(batch):
        n, chunk_at = batch
        await_bytes(gathered.at[chunk_at, 0 : nx - 1], ax_recv.at[n])
        first, count = chunk_at.start * held, (chunk_at.stop - chunk_at.start) * held
        values = gathered[chunk_at].reshape(count, width)
        for i in range(mask_dev // tile):
            lines = slice(i * tile, (i + 1) * tile)
            at = jnp.concatenate([row_at[lines, :] - first] * (count // 128), axis=1)
            pick = (iota((tile, count), 1) == at).astype(F32).astype(BF16)
            put = jnp.dot(pick, values, preferred_element_type=F32)
            if chunk_at.start > 0:
                put = put + grad[lines, :].astype(F32)
            grad[lines, :] = put.astype(BF16)

    def send_losses():
        for d in range(1, ndp):
            loss_copy(d).start()

    def place_losses():
        await_bytes(losses.at[0 : ndp - 1], lo_recv)
        wide = losses[...].reshape(ndp * units, rows)
        high = wide.astype(BF16)
        rest = wide - high.astype(F32)
        middle = rest.astype(BF16)
        low = (rest - middle.astype(F32)).astype(BF16)

        for n in range(mask_dev // tile):
            key = row_key[n * tile : (n + 1) * tile, :]
            line, lane = key // rows, key % rows
            pick = (iota((tile, 128), 1) == line).astype(F32).astype(BF16)[:, : ndp * units]
            lines = sum(
                jnp.dot(pick, part, preferred_element_type=F32) for part in (low, middle, high)
            )
            lane = jnp.concatenate([lane] * (rows // 128), axis=1)
            lines = jnp.where(iota((tile, rows), 1) == lane, lines, 0.0)
            row_loss[:, n * tile : (n + 1) * tile] = jnp.sum(
                jnp.transpose(lines), axis=0, keepdims=True
            )

    pl.semaphore_wait(barrier, len(partners))

    def pipeline(s_exp, t_exp):
        def step(t, carry):
            def at_lag(lag, work, every=1):
                u = t - lag

                @pl.when((u >= 0) & (u < units) & (lax.rem(u, every) == every - 1))
                def _():
                    work(u // every)

            at_lag(0, functools.partial(statistics, s_exp, t_exp))
            at_lag(1, statistics_over_z)
            at_lag(2, statistics_over_far)
            at_lag(DEPTH - 1, functools.partial(gradient, s_exp, t_exp))
            at_lag(DEPTH + 1, gradient_over_z, HALVES)
            at_lag(DEPTH + 3, finish, HALVES)
            return carry

        lax.fori_loop(0, units + DEPTH - 1, step, 0)

    pl.run_scoped(
        pipeline,
        pltpu.VMEM((DEPTH, protos, rows), F32),
        pltpu.VMEM((DEPTH, protos, rows), F32),
    )
    last = chunks - 1
    send_losses()
    early = [(0, slice(0, last - 1))] if last > 1 else []
    before = (1, slice(last - 1, last))
    final = (2, slice(last, chunks))
    for batch in early:
        spread_dp(batch)
    index_rows()
    gradient_over_z(last)
    for batch in early:
        spread_z(batch)
    finish(last - 1)
    spread_dp(before)
    for batch in early:
        spread_x(batch)
    finish(last)
    spread_dp(final)
    spread_z(before)
    spread_z(final)
    spread_x(before)
    for batch in early:
        place(batch)
    place_losses()
    spread_x(final)
    place(before)
    place(final)
    await_bytes(stat_x.at[:, 1:nx], sx_send)
    await_bytes(stat_z.at[:, 1:Z_NEAR], sz_send)
    await_bytes(stat_f.at[:, 1 : nz // Z_NEAR], sf_send)
    await_bytes(got_x.at[:, 1:nx], gx_send)
    await_bytes(got_z.at[:, 1:nz], gz_send)
    await_bytes(got_dp.at[0 : ndp - 1], dp_send)
    await_bytes(gathered.at[:, x, 0 : nz - 1], az_send)
    await_bytes(gathered.at[:, 0 : nx - 1], ax_send)
    await_bytes(losses.at[0 : ndp - 1], lo_send)


def hand_over_kernel(loss, grad, row_loss, student_grad):
    row_loss[...] = loss[...]
    student_grad[0] = grad[...]


def local(ndp, nz, nx, student_rows, teacher_rows, student_proto, teacher_proto, center, counts, order):
    images, patches, width = student_rows.shape
    slots = patches // 2
    protos = student_proto.shape[1]
    chunks = images // nx
    units = chunks * HALVES
    half = slots // HALVES
    rows = nx * half
    piece = slots // nz
    slot_rows = max(8, piece // ndp)
    mask_dev = counts.shape[0] * 96 // ndp
    tile = 256 if mask_dev % 256 == 0 else 128
    dims = (ndp, nz, nx, images, slots, min(512, protos), tile)
    any_spec = pl.BlockSpec(memory_space=pl.ANY)
    vmem = pl.BlockSpec(memory_space=pltpu.VMEM)
    dma = pltpu.SemaphoreType.DMA
    row_loss, grad = pl.pallas_call(
        functools.partial(head_kernel, dims),
        out_shape=(
            jax.ShapeDtypeStruct((1, mask_dev), F32),
            jax.ShapeDtypeStruct((mask_dev, width), BF16),
        ),
        in_specs=[any_spec] * 4 + [vmem] * 3,
        out_specs=(vmem, vmem),
        scratch_shapes=[
            pltpu.VMEM((width, protos), BF16),
            pltpu.VMEM((protos, width), BF16),
            pltpu.VMEM((protos, width), BF16),
            pltpu.VMEM((protos, 128), F32),
            pltpu.VMEM((images, slots, width), BF16),
            pltpu.VMEM((units, nx, half, width), BF16),
            pltpu.VMEM((units, nx, half, width), BF16),
            pltpu.VMEM((units, nx, 4, rows), F32),
            pltpu.VMEM((units, Z_NEAR, 4, rows), F32),
            pltpu.VMEM((units, nz // Z_NEAR, 4, rows), F32),
            pltpu.VMEM((units, nx, half, width), F32),
            pltpu.VMEM((units, nx, half, width), F32),
            pltpu.VMEM((chunks, nz, HALVES, half // nz, width), F32),
            pltpu.VMEM((chunks, nz, HALVES, half // nz, width), F32),
            pltpu.VMEM((ndp, chunks, slot_rows, width), F32),
            pltpu.VMEM((ndp, chunks, slot_rows, width), F32),
            pltpu.VMEM((chunks, nx, nz, piece, width), BF16),
            pltpu.VMEM((ndp, units, rows), F32),
            pltpu.VMEM((mask_dev, 128), jnp.int32),
            pltpu.VMEM((mask_dev, 128), jnp.int32),
            dma((4,)),
            dma, dma((units,)),
            dma, dma((units,)),
            dma, dma((units,)),
            dma, dma((units,)),
            dma, dma((chunks,)),
            dma, dma((3,)),
            dma, dma((3,)),
            dma, dma((3,)),
            dma, dma,
        ],
        compiler_params=pltpu.CompilerParams(
            collective_id=0, has_side_effects=True, vmem_limit_bytes=63 * 2**20
        ),
        name="proto_head",
    )(student_rows, teacher_rows, student_proto, teacher_proto, center[None, :], counts[None, :], order)
    return pl.pallas_call(
        hand_over_kernel,
        out_shape=(
            jax.ShapeDtypeStruct((1, mask_dev), F32),
            jax.ShapeDtypeStruct((1, mask_dev, width), BF16),
        ),
        in_specs=[vmem] * 2,
        out_specs=(vmem, vmem),
        name="hand_over",
    )(row_loss, grad)


def solution(mesh):
    ndp, proto = mesh.shape["dp"], mesh.shape["proto"]
    nx = X_SIZE
    placed = (
        P("dp", None, None),
        P("dp", None, None),
        P(None, "proto"),
        P(None, "proto"),
        P("proto"),
        P(),
        P("dp", None),
    )
    return jax.shard_map(
        functools.partial(local, ndp, proto // nx, nx),
        mesh=mesh,
        in_specs=placed,
        out_specs=(P("dp", None), P("dp", None, None)),
        check_vma=False,
    )
```

```python
import functools
import math

import jax
import jax.numpy as jnp
from jax import lax
from jax.experimental import pallas as pl
from jax.experimental.pallas import tpu as pltpu
from jax.sharding import PartitionSpec as P

STUDENT_TEMP = 0.1
TEACHER_TEMP = 0.07
EPSILON = 1e-06
LOG2E = math.log2(math.e)
X_SIZE = 4
HALVES = 2
DEPTH = 4
F32 = jnp.float32
BF16 = jnp.bfloat16
MESH = pl.DeviceIdType.MESH
NT = (((1,), (1,)), ((), ()))
TN = (((0,), (0,)), ((), ()))


def iota(shape, dim):
    return lax.broadcasted_iota(jnp.int32, shape, dim)


def head_kernel(dims, *refs):
    ndp, nz, nx, images, slots, block, tile = dims
    (student_hbm, teacher_hbm, sproto_hbm, tproto_hbm, center_ref, counts_ref, order_ref,
     row_loss, grad,
     scols, scols_t, tcols_t, center_b, s_in, s_unit, t_unit, stat_x, stat_z, grad_x, got_x,
     grad_z, got_z, own_dp, got_dp, gathered, losses, row_at, row_key,
     load_sem, sx_send, sx_recv, sz_send, sz_recv, gx_send, gx_recv, gz_send, gz_recv,
     dp_send, dp_recv, az_send, az_recv, ax_send, ax_recv, lo_send, lo_recv) = refs
    chunks = images // nx
    units = chunks * HALVES
    half = slots // HALVES
    rows = nx * half
    piece = slots // nz
    unit_piece = half // nz
    per_res = piece // ndp
    slot_rows = own_dp.shape[2]
    protos = scols.shape[1]
    width = scols.shape[0]
    patches = order_ref.shape[1]
    total_images = counts_ref.shape[1]
    mask_dev = grad.shape[0]
    held = nx * nz * piece
    me = lax.axis_index("dp")
    q = lax.axis_index("proto")
    z = q // nx
    x = q % nx

    def along_x(d):
        return (me, z * nx + lax.rem(x + d, nx))

    def along_z(d):
        return (me, lax.rem(z + d, nz) * nx + x)

    def along_dp(d):
        return (lax.rem(me + d, ndp), q)

    barrier = pltpu.get_barrier_semaphore()
    partners = (
        [along_x(d) for d in range(1, nx)]
        + [along_z(d) for d in range(1, nz)]
        + [along_dp(d) for d in range(1, ndp)]
    )
    for partner in partners:
        pl.semaphore_signal(barrier, inc=1, device_id=partner, device_id_type=MESH)

    def prologue(srows, trows, tcols):
        loads = [
            pltpu.make_async_copy(src, dst, load_sem.at[i])
            for i, (src, dst) in enumerate(
                ((student_hbm, srows), (teacher_hbm, trows), (sproto_hbm, scols), (tproto_hbm, tcols))
            )
        ]
        for load in loads:
            load.start()

        def spread_center(n, carry):
            for i in range(spread):
                at = pl.ds(pl.multiple_of((n * spread + i) * 128, 128), 128)
                row = center_ref[:, at] * (LOG2E / TEACHER_TEMP)
                center_b[at, :] = jnp.transpose(jnp.broadcast_to(row, (128, 128)))
            return carry

        def gather_chunk(c, carry):
            for i in range(nx):
                image = c * nx + i
                order = order_ref[pl.ds(image, 1), :][:, :slots]
                pick = (iota((patches, slots), 0) == order).astype(F32).astype(BF16)
                for source, units_ref in ((srows, s_unit), (trows, t_unit)):
                    wide = lax.dot_general(pick, source[image], TN, preferred_element_type=F32)
                    if source is srows:
                        s_in[image] = wide.astype(BF16)
                    norm = jnp.sqrt(jnp.sum(wide * wide, axis=1, keepdims=True) + EPSILON)
                    unit = (wide / norm).reshape(nz, HALVES, unit_piece, width)
                    for h in range(HALVES):
                        units_ref[c * HALVES + h, i] = unit[:, h].reshape(half, width).astype(BF16)
            return carry

        def norm_tiles(n, carry):
            for i in range(group):
                at = pl.ds(pl.multiple_of((n * group + i) * 256, 256), 256)
                for cols, turned in ((scols, scols_t), (tcols, tcols_t)):
                    wide = cols[:, at].astype(F32)
                    scale = 1.0 / jnp.sqrt(jnp.sum(wide * wide, axis=0, keepdims=True) + EPSILON)
                    unit = (wide * scale).astype(BF16)
                    if cols is scols:
                        cols[:, at] = unit
                    turned[at, :] = jnp.transpose(unit)
            return carry

        spread = min(8, protos // 128)
        group = min(4, protos // 256)
        lax.fori_loop(0, protos // (128 * spread), spread_center, 0)
        loads[0].wait()
        loads[1].wait()
        lax.fori_loop(0, chunks, gather_chunk, 0)
        loads[2].wait()
        loads[3].wait()
        lax.fori_loop(0, protos // (256 * group), norm_tiles, 0)

    pl.run_scoped(
        prologue,
        pltpu.VMEM((images, patches, width), BF16),
        pltpu.VMEM((images, patches, width), BF16),
        pltpu.VMEM((width, protos), BF16),
    )

    def copy(src, dst, send, recv, device):
        return pltpu.make_async_remote_copy(
            src_ref=src, dst_ref=dst, send_sem=send, recv_sem=recv, device_id=device,
            device_id_type=MESH,
        )

    def stat_x_copy(c, d):
        return copy(stat_x.at[c, 0], stat_x.at[c, d], sx_send, sx_recv.at[c], along_x(d))

    def stat_z_copy(c, d):
        return copy(stat_z.at[c, 0], stat_z.at[c, d], sz_send, sz_recv.at[c], along_z(d))

    def grad_x_copy(c, d):
        return copy(
            grad_x.at[c, lax.rem(x + d, nx)], got_x.at[c, d], gx_send, gx_recv.at[c], along_x(d)
        )

    def grad_z_copy(c, d):
        return copy(
            grad_z.at[c, lax.rem(z + d, nz)], got_z.at[c, d], gz_send, gz_recv.at[c], along_z(d)
        )

    def dp_copy(batch, d):
        n, at = batch
        return copy(
            own_dp.at[lax.rem(me + d, ndp), at], got_dp.at[me, at], dp_send, dp_recv.at[n],
            along_dp(d),
        )

    def all_z_copy(batch, d):
        n, at = batch
        block_ref = gathered.at[at, x, z]
        return copy(block_ref, block_ref, az_send, az_recv.at[n], along_z(d))

    def all_x_copy(batch, d):
        n, at = batch
        block_ref = gathered.at[at, x]
        return copy(block_ref, block_ref, ax_send, ax_recv.at[n], along_x(d))

    def loss_copy(d):
        return copy(losses.at[me], losses.at[me], lo_send, lo_recv, along_dp(d))

    def await_bytes(ref, sem):
        pltpu.make_async_copy(ref, ref, sem).wait()

    def statistics(s_exp, t_exp, c):
        slot = lax.rem(c, DEPTH)
        student = s_unit[c].reshape(rows, width)
        teacher = t_unit[c].reshape(rows, width)
        sums = [jnp.zeros((8, rows), F32)] * 3
        for n in range(0, protos, block):
            at = pl.ds(n, block)
            s = lax.dot_general(scols_t[at, :], student, NT, preferred_element_type=F32)
            t = lax.dot_general(tcols_t[at, :], teacher, NT, preferred_element_type=F32)
            shift = jnp.concatenate([center_b[at, :]] * (rows // 128), axis=1)
            es = jnp.exp2(s * (LOG2E / STUDENT_TEMP))
            et = jnp.exp2(t * (LOG2E / TEACHER_TEMP) - shift)
            s_exp[slot, at, :] = es
            t_exp[slot, at, :] = et
            sums = [
                total + jnp.sum(part.reshape(block // 8, 8, rows), axis=0)
                for total, part in zip(sums, (es, et, et * s))
            ]
        lines = [jnp.sum(total, axis=0, keepdims=True) for total in sums]
        stat_x[c, 0] = jnp.concatenate(lines + [jnp.zeros((1, rows), F32)], axis=0)
        for d in range(1, nx):
            stat_x_copy(c, d).start()

    def statistics_over_z(c):
        await_bytes(stat_x.at[c, 1:nx], sx_recv.at[c])
        total = stat_x[c, 0]
        for d in range(1, nx):
            total = total + stat_x[c, d]
        stat_z[c, 0] = total
        for d in range(1, nz):
            stat_z_copy(c, d).start()

    def gradient(s_exp, t_exp, c):
        slot = lax.rem(c, DEPTH)
        await_bytes(stat_z.at[c, 1:nz], sz_recv.at[c])
        total = stat_z[c, 0]
        for d in range(1, nz):
            total = total + stat_z[c, d]
        s_sum, t_sum, cross = total[0:1, :], total[1:2, :], total[2:3, :]
        loss = jnp.log(s_sum) - cross * (1.0 / STUDENT_TEMP) / t_sum
        losses[me, pl.ds(c, 1), :] = loss
        s_scale = (1.0 / STUDENT_TEMP) / s_sum
        t_scale = (1.0 / STUDENT_TEMP) / t_sum
        dz = jnp.zeros((width, rows), F32)
        for n in range(0, protos, block):
            at = pl.ds(n, block)
            dlogit = (s_exp[slot, at, :] * s_scale - t_exp[slot, at, :] * t_scale).astype(BF16)
            dz = dz + jnp.dot(scols[:, at], dlogit, preferred_element_type=F32)
        grad_x[c] = jnp.transpose(dz).reshape(nx, half, width)
        for d in range(1, nx):
            grad_x_copy(c, d).start()

    def gradient_over_z(c):
        for h in range(HALVES):
            u = c * HALVES + h
            await_bytes(got_x.at[u, 1:nx], gx_recv.at[u])
            total = grad_x[u, x]
            for d in range(1, nx):
                total = total + got_x[u, d]
            grad_z[c, :, h] = total.reshape(nz, unit_piece, width)
        for d in range(1, nz):
            grad_z_copy(c, d).start()

    def finish(c):
        await_bytes(got_z.at[c, 1:nz], gz_recv.at[c])
        dz = grad_z[c, z]
        for d in range(1, nz):
            dz = dz + got_z[c, d]
        dz = dz.reshape(piece, width)
        image = c * nx + x
        xs = s_in[image, pl.ds(pl.multiple_of(z * piece, piece), piece), :].astype(F32)
        norm = jnp.sqrt(jnp.sum(xs * xs, axis=1, keepdims=True) + EPSILON)
        inner = jnp.sum(xs * dz, axis=1, keepdims=True)
        dx = (dz / norm - xs * inner / (norm * norm * norm)).astype(BF16)
        before = iota(counts_ref.shape, 1) < me * images + image
        start = jnp.sum(jnp.where(before, counts_ref[...].astype(F32), 0.0), axis=1, keepdims=True)
        first = jnp.broadcast_to(start.astype(jnp.int32), (ndp * slot_rows, piece))
        pos = iota((ndp * slot_rows, piece), 0)
        k = iota((ndp * slot_rows, piece), 1)
        pick = (((first + k) % ndp) == pos // slot_rows) & (k // ndp == pos % slot_rows)
        sent = jnp.dot(pick.astype(F32).astype(BF16), dx, preferred_element_type=F32)
        own_dp[:, c] = sent.reshape(ndp, slot_rows, width)
        got_dp[me, c] = own_dp[me, c]

    def spread_dp(batch):
        for d in range(1, ndp):
            dp_copy(batch, d).start()

    def spread_z(batch):
        n, at = batch
        await_bytes(got_dp.at[0 : ndp - 1, at], dp_recv.at[n])
        pos = iota((piece, ndp * slot_rows), 0)
        k = iota((piece, ndp * slot_rows), 1)
        pick = (k // slot_rows == pos // per_res) & (k % slot_rows == pos % per_res)
        pick = pick.astype(F32).astype(BF16)
        for c in range(at.start, at.stop):
            held_rows = got_dp[:, c].reshape(ndp * slot_rows, width).astype(BF16)
            put = jnp.dot(pick, held_rows, preferred_element_type=F32)
            gathered[c, x, z] = put.astype(BF16)
        for d in range(1, nz):
            all_z_copy(batch, d).start()

    def spread_x(batch):
        n, at = batch
        await_bytes(gathered.at[at, x, 0 : nz - 1], az_recv.at[n])
        for d in range(1, nx):
            all_x_copy(batch, d).start()

    def index_rows():
        counts = counts_ref[...].astype(F32)
        upto = iota((total_images, total_images), 0) <= iota((total_images, total_images), 1)
        ends = jnp.dot(
            jnp.broadcast_to(counts, (8, total_images)).astype(BF16),
            upto.astype(F32).astype(BF16), preferred_element_type=F32,
        )[0:1, :]
        starts = ends - counts

        for n in range(mask_dev // tile):
            g = (n * tile + iota((tile, 1), 0)) * ndp + me
            wide = g.astype(F32)
            image = jnp.sum((wide >= ends).astype(F32), axis=1, keepdims=True).astype(jnp.int32)
            start = jnp.max(jnp.where(wide >= starts, starts, 0.0), axis=1, keepdims=True)
            j = g - start.astype(jnp.int32)
            owner, image = image // images, image % images
            at = (image * nz + j // piece) * piece + owner * per_res + (j % piece) // ndp
            lines = slice(n * tile, (n + 1) * tile)
            row_at[lines, :] = jnp.broadcast_to(at, (tile, 128))
            line = owner * units + (image // nx) * HALVES + (j // unit_piece) % HALVES
            lane = (image % nx) * half + (j // piece) * unit_piece + j % unit_piece
            row_key[lines, :] = jnp.broadcast_to(line * rows + lane, (tile, 128))

    def place(batch):
        n, chunk_at = batch
        await_bytes(gathered.at[chunk_at, 0 : nx - 1], ax_recv.at[n])
        first, count = chunk_at.start * held, (chunk_at.stop - chunk_at.start) * held
        values = gathered[chunk_at].reshape(count, width)
        for i in range(mask_dev // tile):
            lines = slice(i * tile, (i + 1) * tile)
            at = jnp.concatenate([row_at[lines, :] - first] * (count // 128), axis=1)
            pick = (iota((tile, count), 1) == at).astype(F32).astype(BF16)
            put = jnp.dot(pick, values, preferred_element_type=F32)
            if chunk_at.start > 0:
                put = put + grad[lines, :].astype(F32)
            grad[lines, :] = put.astype(BF16)

    def send_losses():
        for d in range(1, ndp):
            loss_copy(d).start()

    def place_losses():
        await_bytes(losses.at[0 : ndp - 1], lo_recv)
        wide = losses[...].reshape(ndp * units, rows)
        high = wide.astype(BF16)
        rest = wide - high.astype(F32)
        middle = rest.astype(BF16)
        low = (rest - middle.astype(F32)).astype(BF16)

        for n in range(mask_dev // tile):
            key = row_key[n * tile : (n + 1) * tile, :]
            line, lane = key // rows, key % rows
            pick = (iota((tile, 128), 1) == line).astype(F32).astype(BF16)[:, : ndp * units]
            lines = sum(
                jnp.dot(pick, part, preferred_element_type=F32) for part in (low, middle, high)
            )
            lane = jnp.concatenate([lane] * (rows // 128), axis=1)
            lines = jnp.where(iota((tile, rows), 1) == lane, lines, 0.0)
            row_loss[:, n * tile : (n + 1) * tile] = jnp.sum(
                jnp.transpose(lines), axis=0, keepdims=True
            )

    pl.semaphore_wait(barrier, len(partners))

    def pipeline(s_exp, t_exp):
        def step(t, carry):
            def at_lag(lag, work, every=1):
                u = t - lag

                @pl.when((u >= 0) & (u < units) & (lax.rem(u, every) == every - 1))
                def _():
                    work(u // every)

            at_lag(0, functools.partial(statistics, s_exp, t_exp))
            at_lag(1, statistics_over_z)
            at_lag(DEPTH - 1, functools.partial(gradient, s_exp, t_exp))
            at_lag(DEPTH + 1, gradient_over_z, HALVES)
            at_lag(DEPTH + 3, finish, HALVES)
            return carry

        lax.fori_loop(0, units + DEPTH - 1, step, 0)

    pl.run_scoped(
        pipeline,
        pltpu.VMEM((DEPTH, protos, rows), F32),
        pltpu.VMEM((DEPTH, protos, rows), F32),
    )
    last = chunks - 1
    send_losses()
    early = [(0, slice(0, last - 1))] if last > 1 else []
    before = (1, slice(last - 1, last))
    final = (2, slice(last, chunks))
    for batch in early:
        spread_dp(batch)
    index_rows()
    gradient_over_z(last)
    for batch in early:
        spread_z(batch)
    finish(last - 1)
    spread_dp(before)
    for batch in early:
        spread_x(batch)
    finish(last)
    spread_dp(final)
    spread_z(before)
    spread_z(final)
    spread_x(before)
    for batch in early:
        place(batch)
    place_losses()
    spread_x(final)
    place(before)
    place(final)
    await_bytes(stat_x.at[:, 1:nx], sx_send)
    await_bytes(stat_z.at[:, 1:nz], sz_send)
    await_bytes(got_x.at[:, 1:nx], gx_send)
    await_bytes(got_z.at[:, 1:nz], gz_send)
    await_bytes(got_dp.at[0 : ndp - 1], dp_send)
    await_bytes(gathered.at[:, x, 0 : nz - 1], az_send)
    await_bytes(gathered.at[:, 0 : nx - 1], ax_send)
    await_bytes(losses.at[0 : ndp - 1], lo_send)


def hand_over_kernel(loss, grad, row_loss, student_grad):
    row_loss[...] = loss[...]
    student_grad[0] = grad[...]


def local(ndp, nz, nx, student_rows, teacher_rows, student_proto, teacher_proto, center, counts, order):
    images, patches, width = student_rows.shape
    slots = patches // 2
    protos = student_proto.shape[1]
    chunks = images // nx
    units = chunks * HALVES
    half = slots // HALVES
    rows = nx * half
    piece = slots // nz
    slot_rows = max(8, piece // ndp)
    mask_dev = counts.shape[0] * 96 // ndp
    tile = 256 if mask_dev % 256 == 0 else 128
    dims = (ndp, nz, nx, images, slots, min(512, protos), tile)
    any_spec = pl.BlockSpec(memory_space=pl.ANY)
    vmem = pl.BlockSpec(memory_space=pltpu.VMEM)
    dma = pltpu.SemaphoreType.DMA
    row_loss, grad = pl.pallas_call(
        functools.partial(head_kernel, dims),
        out_shape=(
            jax.ShapeDtypeStruct((1, mask_dev), F32),
            jax.ShapeDtypeStruct((mask_dev, width), BF16),
        ),
        in_specs=[any_spec] * 4 + [vmem] * 3,
        out_specs=(vmem, vmem),
        scratch_shapes=[
            pltpu.VMEM((width, protos), BF16),
            pltpu.VMEM((protos, width), BF16),
            pltpu.VMEM((protos, width), BF16),
            pltpu.VMEM((protos, 128), F32),
            pltpu.VMEM((images, slots, width), BF16),
            pltpu.VMEM((units, nx, half, width), BF16),
            pltpu.VMEM((units, nx, half, width), BF16),
            pltpu.VMEM((units, nx, 4, rows), F32),
            pltpu.VMEM((units, nz, 4, rows), F32),
            pltpu.VMEM((units, nx, half, width), F32),
            pltpu.VMEM((units, nx, half, width), F32),
            pltpu.VMEM((chunks, nz, HALVES, half // nz, width), F32),
            pltpu.VMEM((chunks, nz, HALVES, half // nz, width), F32),
            pltpu.VMEM((ndp, chunks, slot_rows, width), F32),
            pltpu.VMEM((ndp, chunks, slot_rows, width), F32),
            pltpu.VMEM((chunks, nx, nz, piece, width), BF16),
            pltpu.VMEM((ndp, units, rows), F32),
            pltpu.VMEM((mask_dev, 128), jnp.int32),
            pltpu.VMEM((mask_dev, 128), jnp.int32),
            dma((4,)),
            dma, dma((units,)),
            dma, dma((units,)),
            dma, dma((units,)),
            dma, dma((chunks,)),
            dma, dma((3,)),
            dma, dma((3,)),
            dma, dma((3,)),
            dma, dma,
        ],
        compiler_params=pltpu.CompilerParams(
            collective_id=0, has_side_effects=True, vmem_limit_bytes=63 * 2**20
        ),
        name="proto_head",
    )(student_rows, teacher_rows, student_proto, teacher_proto, center[None, :], counts[None, :], order)
    return pl.pallas_call(
        hand_over_kernel,
        out_shape=(
            jax.ShapeDtypeStruct((1, mask_dev), F32),
            jax.ShapeDtypeStruct((1, mask_dev, width), BF16),
        ),
        in_specs=[vmem] * 2,
        out_specs=(vmem, vmem),
        name="hand_over",
    )(row_loss, grad)


def solution(mesh):
    ndp, proto = mesh.shape["dp"], mesh.shape["proto"]
    nx = X_SIZE
    placed = (
        P("dp", None, None),
        P("dp", None, None),
        P(None, "proto"),
        P(None, "proto"),
        P("proto"),
        P(),
        P("dp", None),
    )
    return jax.shard_map(
        functools.partial(local, ndp, proto // nx, nx),
        mesh=mesh,
        in_specs=placed,
        out_specs=(P("dp", None), P("dp", None, None)),
        check_vma=False,
    )
```

```python
import functools
import math

import jax
import jax.numpy as jnp
from jax import lax
from jax.experimental import pallas as pl
from jax.experimental.pallas import tpu as pltpu
from jax.sharding import PartitionSpec as P

STUDENT_TEMP = 0.1
TEACHER_TEMP = 0.07
EPSILON = 1e-06
LOG2E = math.log2(math.e)
X_SIZE = 4
HALVES = 2
DEPTH = 4
F32 = jnp.float32
BF16 = jnp.bfloat16
MESH = pl.DeviceIdType.MESH
NT = (((1,), (1,)), ((), ()))
TN = (((0,), (0,)), ((), ()))


def iota(shape, dim):
    return lax.broadcasted_iota(jnp.int32, shape, dim)


def head_kernel(dims, *refs):
    ndp, nz, nx, images, slots, block, tile = dims
    (student_hbm, teacher_hbm, sproto_hbm, tproto_hbm, center_ref, counts_ref, order_ref,
     row_loss, grad,
     scols, scols_t, tcols_t, center_b, s_in, s_unit, t_unit, stat_x, stat_z, grad_x, got_x,
     grad_z, got_z, own_dp, got_dp, gathered, losses, row_at, row_key,
     load_sem, sx_send, sx_recv, sz_send, sz_recv, gx_send, gx_recv, gz_send, gz_recv,
     dp_send, dp_recv, az_send, az_recv, ax_send, ax_recv, lo_send, lo_recv) = refs
    chunks = images // nx
    units = chunks * HALVES
    half = slots // HALVES
    rows = nx * half
    piece = slots // nz
    unit_piece = half // nz
    per_res = piece // ndp
    slot_rows = own_dp.shape[2]
    protos = scols.shape[1]
    width = scols.shape[0]
    patches = order_ref.shape[1]
    total_images = counts_ref.shape[1]
    mask_dev = grad.shape[0]
    held = nx * nz * piece
    me = lax.axis_index("dp")
    q = lax.axis_index("proto")
    z = q // nx
    x = q % nx

    def along_x(d):
        return (me, z * nx + lax.rem(x + d, nx))

    def along_z(d):
        return (me, lax.rem(z + d, nz) * nx + x)

    def along_dp(d):
        return (lax.rem(me + d, ndp), q)

    barrier = pltpu.get_barrier_semaphore()
    partners = (
        [along_x(d) for d in range(1, nx)]
        + [along_z(d) for d in range(1, nz)]
        + [along_dp(d) for d in range(1, ndp)]
    )
    for partner in partners:
        pl.semaphore_signal(barrier, inc=1, device_id=partner, device_id_type=MESH)

    def prologue(srows, trows, tcols):
        loads = [
            pltpu.make_async_copy(src, dst, load_sem.at[i])
            for i, (src, dst) in enumerate(
                ((student_hbm, srows), (teacher_hbm, trows), (sproto_hbm, scols), (tproto_hbm, tcols))
            )
        ]
        for load in loads:
            load.start()

        def spread_center(n, carry):
            for i in range(spread):
                at = pl.ds(pl.multiple_of((n * spread + i) * 128, 128), 128)
                row = center_ref[:, at] * (LOG2E / TEACHER_TEMP)
                center_b[at, :] = jnp.transpose(jnp.broadcast_to(row, (128, 128)))
            return carry

        def gather_chunk(c, carry):
            for i in range(nx):
                image = c * nx + i
                order = order_ref[pl.ds(image, 1), :][:, :slots]
                pick = (iota((patches, slots), 0) == order).astype(F32).astype(BF16)
                for source, units_ref in ((srows, s_unit), (trows, t_unit)):
                    wide = lax.dot_general(pick, source[image], TN, preferred_element_type=F32)
                    if source is srows:
                        s_in[image] = wide.astype(BF16)
                    norm = jnp.sqrt(jnp.sum(wide * wide, axis=1, keepdims=True) + EPSILON)
                    unit = (wide / norm).reshape(nz, HALVES, unit_piece, width)
                    for h in range(HALVES):
                        units_ref[c * HALVES + h, i] = unit[:, h].reshape(half, width).astype(BF16)
            return carry

        def norm_tiles(n, carry):
            for i in range(group):
                at = pl.ds(pl.multiple_of((n * group + i) * 256, 256), 256)
                for cols, turned in ((scols, scols_t), (tcols, tcols_t)):
                    wide = cols[:, at].astype(F32)
                    scale = 1.0 / jnp.sqrt(jnp.sum(wide * wide, axis=0, keepdims=True) + EPSILON)
                    unit = (wide * scale).astype(BF16)
                    if cols is scols:
                        cols[:, at] = unit
                    turned[at, :] = jnp.transpose(unit)
            return carry

        spread = min(8, protos // 128)
        group = min(4, protos // 256)
        lax.fori_loop(0, protos // (128 * spread), spread_center, 0)
        loads[0].wait()
        loads[1].wait()
        lax.fori_loop(0, chunks, gather_chunk, 0)
        loads[2].wait()
        loads[3].wait()
        lax.fori_loop(0, protos // (256 * group), norm_tiles, 0)

    pl.run_scoped(
        prologue,
        pltpu.VMEM((images, patches, width), BF16),
        pltpu.VMEM((images, patches, width), BF16),
        pltpu.VMEM((width, protos), BF16),
    )

    def copy(src, dst, send, recv, device):
        return pltpu.make_async_remote_copy(
            src_ref=src, dst_ref=dst, send_sem=send, recv_sem=recv, device_id=device,
            device_id_type=MESH,
        )

    def stat_x_copy(c, d):
        return copy(stat_x.at[c, 0], stat_x.at[c, d], sx_send, sx_recv.at[c], along_x(d))

    def stat_z_copy(c, d):
        return copy(stat_z.at[c, 0], stat_z.at[c, d], sz_send, sz_recv.at[c], along_z(d))

    def grad_x_copy(c, d):
        return copy(
            grad_x.at[c, lax.rem(x + d, nx)], got_x.at[c, d], gx_send, gx_recv.at[c], along_x(d)
        )

    def grad_z_copy(c, d):
        return copy(
            grad_z.at[c, lax.rem(z + d, nz)], got_z.at[c, d], gz_send, gz_recv.at[c], along_z(d)
        )

    def dp_copy(batch, d):
        n, at = batch
        return copy(
            own_dp.at[lax.rem(me + d, ndp), at], got_dp.at[me, at], dp_send, dp_recv.at[n],
            along_dp(d),
        )

    def all_z_copy(batch, d):
        n, at = batch
        block_ref = gathered.at[at, x, z]
        return copy(block_ref, block_ref, az_send, az_recv.at[n], along_z(d))

    def all_x_copy(batch, d):
        n, at = batch
        block_ref = gathered.at[at, x]
        return copy(block_ref, block_ref, ax_send, ax_recv.at[n], along_x(d))

    def loss_copy(d):
        return copy(losses.at[me], losses.at[me], lo_send, lo_recv, along_dp(d))

    def await_bytes(ref, sem):
        pltpu.make_async_copy(ref, ref, sem).wait()

    def statistics(s_exp, t_exp, c):
        slot = lax.rem(c, DEPTH)
        student = s_unit[c].reshape(rows, width)
        teacher = t_unit[c].reshape(rows, width)
        sums = [jnp.zeros((8, rows), F32)] * 3
        for n in range(0, protos, block):
            at = pl.ds(n, block)
            s = lax.dot_general(scols_t[at, :], student, NT, preferred_element_type=F32)
            t = lax.dot_general(tcols_t[at, :], teacher, NT, preferred_element_type=F32)
            shift = jnp.concatenate([center_b[at, :]] * (rows // 128), axis=1)
            es = jnp.exp2(s * (LOG2E / STUDENT_TEMP))
            et = jnp.exp2(t * (LOG2E / TEACHER_TEMP) - shift)
            s_exp[slot, at, :] = es
            t_exp[slot, at, :] = et
            sums = [
                total + jnp.sum(part.reshape(block // 8, 8, rows), axis=0)
                for total, part in zip(sums, (es, et, et * s))
            ]
        lines = [jnp.sum(total, axis=0, keepdims=True) for total in sums]
        stat_x[c, 0] = jnp.concatenate(lines + [jnp.zeros((1, rows), F32)], axis=0)
        for d in range(1, nx):
            stat_x_copy(c, d).start()

    def statistics_over_z(c):
        await_bytes(stat_x.at[c, 1:nx], sx_recv.at[c])
        total = stat_x[c, 0]
        for d in range(1, nx):
            total = total + stat_x[c, d]
        stat_z[c, 0] = total
        for d in range(1, nz):
            stat_z_copy(c, d).start()

    def gradient(s_exp, t_exp, c):
        slot = lax.rem(c, DEPTH)
        await_bytes(stat_z.at[c, 1:nz], sz_recv.at[c])
        total = stat_z[c, 0]
        for d in range(1, nz):
            total = total + stat_z[c, d]
        s_sum, t_sum, cross = total[0:1, :], total[1:2, :], total[2:3, :]
        loss = jnp.log(s_sum) - cross * (1.0 / STUDENT_TEMP) / t_sum
        losses[me, pl.ds(c, 1), :] = loss
        s_scale = (1.0 / STUDENT_TEMP) / s_sum
        t_scale = (1.0 / STUDENT_TEMP) / t_sum
        dz = jnp.zeros((width, rows), F32)
        for n in range(0, protos, block):
            at = pl.ds(n, block)
            dlogit = (s_exp[slot, at, :] * s_scale - t_exp[slot, at, :] * t_scale).astype(BF16)
            dz = dz + jnp.dot(scols[:, at], dlogit, preferred_element_type=F32)
        grad_x[c] = jnp.transpose(dz).reshape(nx, half, width)
        for d in range(1, nx):
            grad_x_copy(c, d).start()

    def gradient_over_z(c):
        for h in range(HALVES):
            u = c * HALVES + h
            await_bytes(got_x.at[u, 1:nx], gx_recv.at[u])
            total = grad_x[u, x]
            for d in range(1, nx):
                total = total + got_x[u, d]
            grad_z[c, :, h] = total.reshape(nz, unit_piece, width)
        for d in range(1, nz):
            grad_z_copy(c, d).start()

    def finish(c):
        await_bytes(got_z.at[c, 1:nz], gz_recv.at[c])
        dz = grad_z[c, z]
        for d in range(1, nz):
            dz = dz + got_z[c, d]
        dz = dz.reshape(piece, width)
        image = c * nx + x
        xs = s_in[image, pl.ds(pl.multiple_of(z * piece, piece), piece), :].astype(F32)
        norm = jnp.sqrt(jnp.sum(xs * xs, axis=1, keepdims=True) + EPSILON)
        inner = jnp.sum(xs * dz, axis=1, keepdims=True)
        dx = (dz / norm - xs * inner / (norm * norm * norm)).astype(BF16)
        before = iota(counts_ref.shape, 1) < me * images + image
        start = jnp.sum(jnp.where(before, counts_ref[...].astype(F32), 0.0), axis=1, keepdims=True)
        first = jnp.broadcast_to(start.astype(jnp.int32), (ndp * slot_rows, piece))
        pos = iota((ndp * slot_rows, piece), 0)
        k = iota((ndp * slot_rows, piece), 1)
        pick = (((first + k) % ndp) == pos // slot_rows) & (k // ndp == pos % slot_rows)
        sent = jnp.dot(pick.astype(F32).astype(BF16), dx, preferred_element_type=F32)
        own_dp[:, c] = sent.reshape(ndp, slot_rows, width)
        got_dp[me, c] = own_dp[me, c]

    def spread_dp(batch):
        for d in range(1, ndp):
            dp_copy(batch, d).start()

    def spread_z(batch):
        n, at = batch
        await_bytes(got_dp.at[0 : ndp - 1, at], dp_recv.at[n])
        pos = iota((piece, ndp * slot_rows), 0)
        k = iota((piece, ndp * slot_rows), 1)
        pick = (k // slot_rows == pos // per_res) & (k % slot_rows == pos % per_res)
        pick = pick.astype(F32).astype(BF16)
        for c in range(at.start, at.stop):
            held_rows = got_dp[:, c].reshape(ndp * slot_rows, width).astype(BF16)
            put = jnp.dot(pick, held_rows, preferred_element_type=F32)
            gathered[c, x, z] = put.astype(BF16)
        for d in range(1, nz):
            all_z_copy(batch, d).start()

    def spread_x(batch):
        n, at = batch
        await_bytes(gathered.at[at, x, 0 : nz - 1], az_recv.at[n])
        for d in range(1, nx):
            all_x_copy(batch, d).start()

    def index_rows():
        counts = counts_ref[...].astype(F32)
        upto = iota((total_images, total_images), 0) <= iota((total_images, total_images), 1)
        ends = jnp.dot(
            jnp.broadcast_to(counts, (8, total_images)).astype(BF16),
            upto.astype(F32).astype(BF16), preferred_element_type=F32,
        )[0:1, :]
        starts = ends - counts

        for n in range(mask_dev // tile):
            g = (n * tile + iota((tile, 1), 0)) * ndp + me
            wide = g.astype(F32)
            image = jnp.sum((wide >= ends).astype(F32), axis=1, keepdims=True).astype(jnp.int32)
            start = jnp.max(jnp.where(wide >= starts, starts, 0.0), axis=1, keepdims=True)
            j = g - start.astype(jnp.int32)
            owner, image = image // images, image % images
            at = (image * nz + j // piece) * piece + owner * per_res + (j % piece) // ndp
            lines = slice(n * tile, (n + 1) * tile)
            row_at[lines, :] = jnp.broadcast_to(at, (tile, 128))
            line = owner * units + (image // nx) * HALVES + (j // unit_piece) % HALVES
            lane = (image % nx) * half + (j // piece) * unit_piece + j % unit_piece
            row_key[lines, :] = jnp.broadcast_to(line * rows + lane, (tile, 128))

    def place(batch):
        n, chunk_at = batch
        await_bytes(gathered.at[chunk_at, 0 : nx - 1], ax_recv.at[n])
        first, count = chunk_at.start * held, (chunk_at.stop - chunk_at.start) * held
        values = gathered[chunk_at].reshape(count, width)
        for i in range(mask_dev // tile):
            lines = slice(i * tile, (i + 1) * tile)
            at = jnp.concatenate([row_at[lines, :] - first] * (count // 128), axis=1)
            pick = (iota((tile, count), 1) == at).astype(F32).astype(BF16)
            put = jnp.dot(pick, values, preferred_element_type=F32)
            if chunk_at.start > 0:
                put = put + grad[lines, :].astype(F32)
            grad[lines, :] = put.astype(BF16)

    def send_losses():
        for d in range(1, ndp):
            loss_copy(d).start()

    def place_losses():
        await_bytes(losses.at[0 : ndp - 1], lo_recv)
        wide = losses[...].reshape(ndp * units, rows)
        high = wide.astype(BF16)
        rest = wide - high.astype(F32)
        middle = rest.astype(BF16)
        low = (rest - middle.astype(F32)).astype(BF16)

        for n in range(mask_dev // tile):
            key = row_key[n * tile : (n + 1) * tile, :]
            line, lane = key // rows, key % rows
            pick = (iota((tile, 128), 1) == line).astype(F32).astype(BF16)[:, : ndp * units]
            lines = sum(
                jnp.dot(pick, part, preferred_element_type=F32) for part in (low, middle, high)
            )
            lane = jnp.concatenate([lane] * (rows // 128), axis=1)
            lines = jnp.where(iota((tile, rows), 1) == lane, lines, 0.0)
            row_loss[:, n * tile : (n + 1) * tile] = jnp.sum(
                jnp.transpose(lines), axis=0, keepdims=True
            )

    pl.semaphore_wait(barrier, len(partners))

    def pipeline(s_exp, t_exp):
        def step(t, carry):
            def at_lag(lag, work, every=1):
                u = t - lag

                @pl.when((u >= 0) & (u < units) & (lax.rem(u, every) == every - 1))
                def _():
                    work(u // every)

            at_lag(0, functools.partial(statistics, s_exp, t_exp))
            at_lag(1, statistics_over_z)
            at_lag(DEPTH - 1, functools.partial(gradient, s_exp, t_exp))
            at_lag(DEPTH + 1, gradient_over_z, HALVES)
            at_lag(DEPTH + 3, finish, HALVES)
            return carry

        lax.fori_loop(0, units + DEPTH - 1, step, 0)

    pl.run_scoped(
        pipeline,
        pltpu.VMEM((DEPTH, protos, rows), F32),
        pltpu.VMEM((DEPTH, protos, rows), F32),
    )
    last = chunks - 1
    send_losses()
    early = [(0, slice(0, last - 1))] if last > 1 else []
    before = (1, slice(last - 1, last))
    final = (2, slice(last, chunks))
    for batch in early:
        spread_dp(batch)
    index_rows()
    gradient_over_z(last)
    for batch in early:
        spread_z(batch)
    finish(last - 1)
    spread_dp(before)
    for batch in early:
        spread_x(batch)
    finish(last)
    spread_dp(final)
    spread_z(before)
    spread_z(final)
    spread_x(before)
    for batch in early:
        place(batch)
    spread_x(final)
    place_losses()
    place(before)
    place(final)
    await_bytes(stat_x.at[:, 1:nx], sx_send)
    await_bytes(stat_z.at[:, 1:nz], sz_send)
    await_bytes(got_x.at[:, 1:nx], gx_send)
    await_bytes(got_z.at[:, 1:nz], gz_send)
    await_bytes(got_dp.at[0 : ndp - 1], dp_send)
    await_bytes(gathered.at[:, x, 0 : nz - 1], az_send)
    await_bytes(gathered.at[:, 0 : nx - 1], ax_send)
    await_bytes(losses.at[0 : ndp - 1], lo_send)


def hand_over_kernel(loss, grad, row_loss, student_grad):
    row_loss[...] = loss[...]
    student_grad[0] = grad[...]


def local(ndp, nz, nx, student_rows, teacher_rows, student_proto, teacher_proto, center, counts, order):
    images, patches, width = student_rows.shape
    slots = patches // 2
    protos = student_proto.shape[1]
    chunks = images // nx
    units = chunks * HALVES
    half = slots // HALVES
    rows = nx * half
    piece = slots // nz
    slot_rows = max(8, piece // ndp)
    mask_dev = counts.shape[0] * 96 // ndp
    tile = 256 if mask_dev % 256 == 0 else 128
    dims = (ndp, nz, nx, images, slots, min(512, protos), tile)
    any_spec = pl.BlockSpec(memory_space=pl.ANY)
    vmem = pl.BlockSpec(memory_space=pltpu.VMEM)
    dma = pltpu.SemaphoreType.DMA
    row_loss, grad = pl.pallas_call(
        functools.partial(head_kernel, dims),
        out_shape=(
            jax.ShapeDtypeStruct((1, mask_dev), F32),
            jax.ShapeDtypeStruct((mask_dev, width), BF16),
        ),
        in_specs=[any_spec] * 4 + [vmem] * 3,
        out_specs=(vmem, vmem),
        scratch_shapes=[
            pltpu.VMEM((width, protos), BF16),
            pltpu.VMEM((protos, width), BF16),
            pltpu.VMEM((protos, width), BF16),
            pltpu.VMEM((protos, 128), F32),
            pltpu.VMEM((images, slots, width), BF16),
            pltpu.VMEM((units, nx, half, width), BF16),
            pltpu.VMEM((units, nx, half, width), BF16),
            pltpu.VMEM((units, nx, 4, rows), F32),
            pltpu.VMEM((units, nz, 4, rows), F32),
            pltpu.VMEM((units, nx, half, width), F32),
            pltpu.VMEM((units, nx, half, width), F32),
            pltpu.VMEM((chunks, nz, HALVES, half // nz, width), F32),
            pltpu.VMEM((chunks, nz, HALVES, half // nz, width), F32),
            pltpu.VMEM((ndp, chunks, slot_rows, width), F32),
            pltpu.VMEM((ndp, chunks, slot_rows, width), F32),
            pltpu.VMEM((chunks, nx, nz, piece, width), BF16),
            pltpu.VMEM((ndp, units, rows), F32),
            pltpu.VMEM((mask_dev, 128), jnp.int32),
            pltpu.VMEM((mask_dev, 128), jnp.int32),
            dma((4,)),
            dma, dma((units,)),
            dma, dma((units,)),
            dma, dma((units,)),
            dma, dma((chunks,)),
            dma, dma((3,)),
            dma, dma((3,)),
            dma, dma((3,)),
            dma, dma,
        ],
        compiler_params=pltpu.CompilerParams(
            collective_id=0, has_side_effects=True, vmem_limit_bytes=63 * 2**20
        ),
        name="proto_head",
    )(student_rows, teacher_rows, student_proto, teacher_proto, center[None, :], counts[None, :], order)
    return pl.pallas_call(
        hand_over_kernel,
        out_shape=(
            jax.ShapeDtypeStruct((1, mask_dev), F32),
            jax.ShapeDtypeStruct((1, mask_dev, width), BF16),
        ),
        in_specs=[vmem] * 2,
        out_specs=(vmem, vmem),
        name="hand_over",
    )(row_loss, grad)


def solution(mesh):
    ndp, proto = mesh.shape["dp"], mesh.shape["proto"]
    nx = X_SIZE
    placed = (
        P("dp", None, None),
        P("dp", None, None),
        P(None, "proto"),
        P(None, "proto"),
        P("proto"),
        P(),
        P("dp", None),
    )
    return jax.shard_map(
        functools.partial(local, ndp, proto // nx, nx),
        mesh=mesh,
        in_specs=placed,
        out_specs=(P("dp", None), P("dp", None, None)),
        check_vma=False,
    )
```
